256 devices in a mesh: rows: 8 (over z), hidden: 32 (over x, y, core).
Axes of the slice: x: 4, y: 4, z: 8, core: 2. Of those that a mesh axis runs over, the one named last changes fastest.
Arguments:
- tokens: bfloat16 [1024, 8192], P('hidden', 'rows'), may hold values from -6 to 6
- snapshot: int32 [1024, 1], replicated, may hold values from 0 to 63; in each aligned block of 1024 rows (0 to 1023, 1024 to 2047, ...) at most 32 rows name the same one
- gate_weight: bfloat16 [8192, 28672], P('rows', 'hidden'), may hold values from -0.0625 to 0.0625
- up_weight: bfloat16 [8192, 28672], P('rows', 'hidden'), may hold values from -0.0625 to 0.0625
- down_weight: bfloat16 [28672, 8192], P('hidden', 'rows'), may hold values from -0.03125 to 0.03125
- adapter_input_maps: bfloat16 [64, 8192, 128], P('hidden', 'rows')
- adapter_middle_maps: bfloat16 [64, 2, 64, 28672], P(None, None, 'rows', 'hidden'), may hold values from -0.375 to 0.375
- down_input_map: bfloat16 [64, 64, 28672], P(None, 'rows', 'hidden')
- down_output_map: bfloat16 [64, 64, 8192], P('hidden', None, 'rows'), may hold values from -0.75 to 0.75
Outputs:
- mixed: bfloat16 [1024, 8192], P('hidden', 'rows')
The draws below stay inside these ranges and needn't reach their ends.
Inputs may be any that keep to these rules, and one draw needn't show every extreme that they name: Every snapshot is named by at least one row and by at most 32 rows; some snapshot is named by exactly 32 rows.
All inputs are finite; a program needn't handle non-finite values.
Results may differ from the reference program's by a relative error of at most 0.033.
Values may be sent and summed in bfloat16 or wider, within the bound.
No kernel may reach another device: no remote copies, remote signals or barrier semaphores. Data moves between devices by JAX's collectives and lax.ppermute only.
A program may use at most 128 MiB of HBM per device.

```python
import math
import jax
import jax.numpy as jnp
import numpy as np
from jax import lax

MODEL_WIDTH = 8192
HIDDEN_UNITS = 28672
ADAPTER_RANK = 64
SNAP_DEV = 2
SNAPSHOT_COUNT = 64
TOKENS = 1024
CAP = 32
GROUPS = 8
DBLK = 1024
RANK_BLOCK_SIZE = 8
N_ROWS = 8
N_HIDDEN = 32


def unit_noise(key, shape):
    return jax.random.normal(key, shape, jnp.float32)


def draw_adapter_input_maps(key, part):
    key = jax.random.fold_in(key, 11)
    width_block = MODEL_WIDTH // N_ROWS
    rank_block = ADAPTER_RANK // N_ROWS
    feature_group = jnp.arange(MODEL_WIDTH, dtype=jnp.int32) // width_block
    column_group = jnp.arange(2 * ADAPTER_RANK, dtype=jnp.int32) % ADAPTER_RANK // rank_block
    paired = feature_group[:, None] == (column_group[None, :] + N_ROWS // 2) % N_ROWS
    factor = jnp.where(paired, 6.0, 1.0).astype(jnp.float32)
    noise = unit_noise(key, (SNAPSHOT_COUNT, MODEL_WIDTH, 2 * ADAPTER_RANK))
    return (noise * factor[None, :, :] * MODEL_WIDTH ** (-0.5)).astype(jnp.bfloat16)


def draw_down_input_map(key, part):
    key = jax.random.fold_in(key, 23)
    unit_block = HIDDEN_UNITS // N_HIDDEN
    owner_group = jnp.arange(SNAPSHOT_COUNT, dtype=jnp.int32) // SNAP_DEV
    unit_group = jnp.arange(HIDDEN_UNITS, dtype=jnp.int32) // unit_block
    paired = owner_group[:, None] == unit_group[None, :]
    factor = jnp.where(paired, 6.0, 1.0).astype(jnp.float32)
    noise = unit_noise(key, (SNAPSHOT_COUNT, ADAPTER_RANK, HIDDEN_UNITS))
    return (noise * factor[:, None, :] * HIDDEN_UNITS ** (-0.5)).astype(jnp.bfloat16)


def block_levels(rng, extent, split, low, top_value):
    loudness, own = 1.0, jax.random.fold_in(rng, 6)
    for dim, shards_of in split:
        draws = jnp.exp(jax.random.uniform(jax.random.fold_in(own, dim), (shards_of,), jnp.float32, low / len(split), top_value / len(split)))
        loudness = loudness * jnp.repeat(draws, extent[dim] // shards_of).reshape([-1 if axis == dim else 1 for axis in range(len(extent))])
    return loudness


def deal_out(own_key, own, number, rows, amount, top, most, skew):
    order = jax.random.permutation(own_key, amount)
    packed, common = portions_of(amount, rows * top, most, skew, True), portions_of(amount, rows * top, most, skew, False)
    places = jnp.arange(amount)

    def named(sizes, turn):
        used = int((sizes > 0).sum())
        fixed = max(1, used // 4)
        shifted = fixed + (places - fixed + turn * (used - fixed)) % max(1, amount - fixed)
        return jnp.zeros((amount,), jnp.int32).at[order[jnp.where(places < fixed, places, shifted)]].set(jnp.asarray(sizes, jnp.int32))

    sizes = jnp.where(number % 4 == 0, named(packed, number // 4), named(common, number - number // 4 - 1))
    mixed = jax.random.permutation(jax.random.fold_in(own, 3), amount)
    giver, receiver = mixed[0:amount // 2 * 2:2], mixed[1:amount // 2 * 2:2]
    room = jnp.minimum(sizes[giver] - 1, most - sizes[receiver]) // 2
    room = jnp.where((giver == order[0]) | (receiver == order[0]) | (sizes[receiver] == 0), 0, jnp.maximum(room, 0))
    shifted = jax.random.randint(jax.random.fold_in(own, 4), (amount // 2,), 0, 1 << 20) % (room + 1)
    sizes = sizes.at[giver].add(-shifted).at[receiver].add(shifted)
    members = jnp.searchsorted(jnp.cumsum(sizes), jnp.arange(rows * top), side="right").astype(jnp.int32)
    table = members.reshape(top, rows).T
    table = table[jax.random.permutation(jax.random.fold_in(own, 1), rows)]
    turn = jax.random.randint(jax.random.fold_in(own, 2), (rows, 1), 0, top)
    return jnp.take_along_axis(table, (jnp.arange(top)[None, :] + turn) % top, axis=1)


def portions_of(count, total, bound, lean, full):
    weights = [(1 << 20) // math.isqrt(standing ** lean) + 1 for standing in range(1, count + 1)]
    largest = bound if full else min(bound, max(-(-total // count), total * weights[0] // sum(weights)))
    least = 1 if total - largest >= count - 1 else 0
    holding, spare = [largest] + [least] * (count - 1), total - largest - least * (count - 1)
    while spare > 0:
        candidates = [i for i in range(1, count) if holding[i] < largest] or [i for i in range(1, count) if holding[i] < bound]
        whole, left = sum([weights[i] for i in candidates]), spare
        for i in candidates:
            more = min(bound - holding[i], max(1, left * weights[i] // whole), spare)
            holding[i] = holding[i] + more
            spare = spare - more
    return np.array(holding)


def scatter_about(own_key, dims, spread, reach, pieces=(), held_as=jnp.bfloat16):
    result = spread * jax.random.normal(own_key, dims, jnp.float32)
    if pieces:
        result = result * block_levels(own_key, dims, pieces, -0.22, 0.18)
    return jnp.clip(result, -reach, reach).astype(held_as)


def setup_inputs(seed: int = 0) -> dict:
    key_list = jax.random.split(jax.random.key(seed), 10)
    tokens = scatter_about(key_list[0], (TOKENS, MODEL_WIDTH), 1.0, 6.0, ((0, 32), (1, 8)))
    snapshot_keys = jax.random.split(jax.random.fold_in(key_list[1], 1), TOKENS // TOKENS)
    snapshot_turns = jax.random.permutation(jax.random.fold_in(key_list[1], 3), TOKENS // TOKENS)
    snapshot = jax.vmap(lambda own, number: deal_out(jax.random.fold_in(key_list[1], 2), own, number, TOKENS, SNAPSHOT_COUNT, 1, CAP, 2))(snapshot_keys, snapshot_turns).reshape((TOKENS, 1))
    gate_weight = scatter_about(key_list[2], (MODEL_WIDTH, HIDDEN_UNITS), MODEL_WIDTH ** -0.5, 0.0625, ((0, 8), (1, 32)))
    up_weight = scatter_about(key_list[3], (MODEL_WIDTH, HIDDEN_UNITS), MODEL_WIDTH ** -0.5, 0.0625, ((0, 8), (1, 32)))
    down_weight = scatter_about(key_list[4], (HIDDEN_UNITS, MODEL_WIDTH), HIDDEN_UNITS ** -0.5, 0.03125, ((0, 32), (1, 8)))
    adapter_input_maps = draw_adapter_input_maps(jax.random.fold_in(key_list[9], 71), 0)
    adapter_middle_maps = scatter_about(key_list[6], (SNAPSHOT_COUNT, 2, ADAPTER_RANK, HIDDEN_UNITS), (4 * ADAPTER_RANK) ** -0.5, 0.375, ((2, 8), (3, 32)))
    down_input_map = draw_down_input_map(jax.random.fold_in(key_list[9], 71), 0)
    down_output_map = scatter_about(key_list[8], (SNAPSHOT_COUNT, ADAPTER_RANK, MODEL_WIDTH), ADAPTER_RANK ** -0.5, 0.75, ((0, 32), (2, 8)))
    return {"tokens": tokens, "snapshot": snapshot, "gate_weight": gate_weight, "up_weight": up_weight, "down_weight": down_weight, "adapter_input_maps": adapter_input_maps, "adapter_middle_maps": adapter_middle_maps, "down_input_map": down_input_map, "down_output_map": down_output_map}


def slot_tables(snapshot, snapshot_total, capacity):
    row_total = snapshot.shape[0]
    snap_owner = snapshot[:, 0].astype(jnp.int32)
    onehot = (snap_owner[:, None] == jnp.arange(snapshot_total, dtype=jnp.int32)[None, :]).astype(jnp.int32)
    before = jnp.cumsum(onehot, axis=0) - onehot
    slot_index = jnp.sum(before * onehot, axis=1).astype(jnp.int32)
    token_of = jnp.full((snapshot_total, capacity), row_total, jnp.int32)
    token_of = token_of.at[snap_owner, slot_index].set(jnp.arange(row_total, dtype=jnp.int32))
    return snap_owner, slot_index, token_of


def narrow_product(inputs):
    left_side, right_side = inputs
    return jnp.dot(left_side, right_side, preferred_element_type=jnp.float32)


def reference(tokens, snapshot, gate_weight, up_weight, down_weight, adapter_input_maps, adapter_middle_maps, down_input_map, down_output_map):
    snap_owner, slot_index, token_of = slot_tables(snapshot, SNAPSHOT_COUNT, CAP)
    filled_flag = token_of < TOKENS
    clamped_index = jnp.minimum(token_of, TOKENS - 1)

    def rank_input_values(inputs):
        row_ids, filled_rows, weight = inputs
        picked_snapshot = jnp.where(filled_rows[:, None], tokens[row_ids], jnp.zeros((), tokens.dtype))
        return jnp.dot(picked_snapshot, weight, preferred_element_type=jnp.float32)

    rank_activation_values = lax.map(rank_input_values, (clamped_index, filled_flag, adapter_input_maps)).astype(jnp.bfloat16)
    rank_activation_values = rank_activation_values.reshape(SNAPSHOT_COUNT, CAP, 2, ADAPTER_RANK)
    gate_up = jnp.zeros((TOKENS, 2, HIDDEN_UNITS), jnp.float32)
    for block_index in range(GROUPS):
        feature_lo = block_index * DBLK
        rank_lower_start = block_index * RANK_BLOCK_SIZE
        token_block = tokens[:, feature_lo:feature_lo + DBLK]
        summands = []
        for half_position, weight in enumerate((gate_weight, up_weight)):
            base_term = jnp.dot(token_block, weight[feature_lo:feature_lo + DBLK], preferred_element_type=jnp.float32)
            grouped_rows = lax.map(narrow_product, (rank_activation_values[:, :, half_position, rank_lower_start:rank_lower_start + RANK_BLOCK_SIZE], adapter_middle_maps[:, half_position, rank_lower_start:rank_lower_start + RANK_BLOCK_SIZE, :]))
            summands.append(base_term + grouped_rows[snap_owner, slot_index])
        partial_value = jnp.stack(summands, axis=1).astype(jnp.bfloat16)
        partial_value = lax.optimization_barrier(partial_value)
        gate_up = gate_up + partial_value.astype(jnp.float32)
    hidden = (jax.nn.silu(gate_up[:, 0]) * gate_up[:, 1]).astype(jnp.bfloat16)

    def rank_down(inputs):
        row_ids, filled_rows, weight = inputs
        picked_snapshot = jnp.where(filled_rows[:, None], hidden[row_ids], jnp.zeros((), hidden.dtype))
        return jnp.dot(picked_snapshot, weight.T, preferred_element_type=jnp.float32)

    down_rank = lax.map(rank_down, (clamped_index, filled_flag, down_input_map)).astype(jnp.bfloat16)
    lifted = lax.map(narrow_product, (down_rank, down_output_map))
    base_out = jnp.dot(hidden, down_weight, preferred_element_type=jnp.float32)
    return (base_out + lifted[snap_owner, slot_index]).astype(jnp.bfloat16)
```

```python
import jax
import jax.numpy as jnp
from jax import lax
from jax.experimental import pallas as pl
from jax.experimental.pallas import tpu as pltpu
from jax.sharding import PartitionSpec as P

BF = jnp.bfloat16
F32 = jnp.float32
NX, NY, NZ = 4, 4, 8
ROWS, HID = "rows", "hidden"


def _h(x, y, c):
    return (x * NY + y) * 2 + c


def _plane(f):
    return [
        (_h(x, y, c), _h(*f(x, y, c))) for x in range(NX) for y in range(NY) for c in range(2)
    ]


def _on_x(k):
    return lambda x, y, c: ((x + k) % NX, y, c)


def _on_y(k):
    return lambda x, y, c: (x, (y + k) % NY, c)


FIRST = {k: _plane(lambda x, y, c, k=k: (_on_y(k) if c else _on_x(k))(x, y, c)) for k in (1, 2, 3)}
SECOND = {k: _plane(lambda x, y, c, k=k: (_on_x(k) if c else _on_y(k))(x, y, c)) for k in (1, 2, 3)}
SIBLING = _plane(lambda x, y, c: (x, y, 1 - c))
UP_Z = [(i, (i + 1) % NZ) for i in range(NZ)]
DOWN_Z = [(i, (i - 1) % NZ) for i in range(NZ)]


def _params(mib):
    return pltpu.CompilerParams(vmem_limit_bytes=mib << 20)


def _dot(a, b):
    return jnp.dot(a, b, preferred_element_type=F32)


def _dot_nt(a, b):
    return lax.dot_general(a, b, (((1,), (1,)), ((), ())), preferred_element_type=F32)


VM = pl.BlockSpec(memory_space=pltpu.VMEM)
ANY = pl.BlockSpec(memory_space=pl.ANY)
SM = pl.BlockSpec(memory_space=pltpu.SMEM)


def rank_kernel(pick_ref, own_ref, sib_ref, maps_ref, out_ref):
    half = own_ref.shape[0]
    picked = _dot(pick_ref[:, :half], own_ref[...]) + _dot(pick_ref[:, half:], sib_ref[...])
    picked = picked.astype(BF)
    cap = picked.shape[0] // 2
    ranks = jnp.concatenate(
        [_dot(picked[i * cap : (i + 1) * cap], maps_ref[i]) for i in range(2)], axis=0
    )
    turned = ranks.T
    blocks, k = out_ref.shape[0], out_ref.shape[1]
    side = blocks * k
    out_ref[...] = jnp.concatenate(
        [turned[:side].reshape(blocks, k, 2 * cap), turned[side:].reshape(blocks, k, 2 * cap)],
        axis=2,
    )


def up_kernel(
    place_ref, snap_ref, slot_ref, ranks_ref, own_ref, sib_ref, gate_ref, up_ref, mid_ref, out_ref,
    rows_ref, gate_v, up_v, mid_v, sems, row_sems,
):
    weights = [
        pltpu.make_async_copy(gate_ref, gate_v, sems.at[0]),
        pltpu.make_async_copy(up_ref, up_v, sems.at[1]),
        pltpu.make_async_copy(mid_ref, mid_v, sems.at[2]),
    ]
    moves = []
    for p in range(32):
        source = own_ref if p < 16 else sib_ref
        moves.append(
            pltpu.make_async_copy(
                source.at[pl.ds((p % 16) * 32, 32)],
                rows_ref.at[pl.ds(pl.multiple_of(place_ref[p] * 32, 32), 32)],
                row_sems.at[p],
            )
        )
    for copy in moves + weights:
        copy.start()
    for copy in moves + weights:
        copy.wait()
    block = 256
    ranks = ranks_ref[...]

    def body(i, carry):
        at = pl.ds(pl.multiple_of(i * block, block), block)
        rows = rows_ref[at, :]
        snap = snap_ref[at, :]
        slot = slot_ref[at, :]
        lane = lax.broadcasted_iota(jnp.int32, (block, 128), 1)
        column = lax.broadcasted_iota(jnp.int32, (block, 256), 1)
        for j in range(2):
            spread = []
            for l in range(2):
                hot = jnp.where(lane == slot + 32 * (2 * j + l), 1.0, 0.0).astype(BF)
                wide = _dot_nt(hot, ranks)
                spread.append(jnp.where(2 * (column // 8) + l == snap, wide, 0.0).astype(BF))
            total = _dot(rows, (up_v if j else gate_v)[...])
            total += _dot(jnp.concatenate(spread, axis=1), mid_v[j])
            out_ref[j, at, :] = total.astype(BF)
        return carry

    lax.fori_loop(0, rows_ref.shape[0] // block, body, 0)


def down_kernel(
    place_ref, owner_ref, snap_ref, *rest
):
    pieces = rest[:9]
    weight_ref, map_ref, out_ref, rank_ref, hid_v, weight_v, map_v, sems = rest[9:]
    copies, row = [], 0
    for n, piece in enumerate(pieces):
        copies.append(
            pltpu.make_async_copy(piece, hid_v.at[pl.ds(row, piece.shape[0])], sems.at[n])
        )
        row += piece.shape[0]
    copies.append(pltpu.make_async_copy(map_ref, map_v, sems.at[9]))
    copies.append(pltpu.make_async_copy(weight_ref, weight_v, sems.at[10]))
    for copy in copies:
        copy.start()
    for copy in copies:
        copy.wait()
    block = 256

    def body(i, carry):
        at = pl.ds(pl.multiple_of(i * block, block), block)
        hidden = hid_v[at, :]
        wide = _dot_nt(map_v[...], hidden)
        snap = snap_ref[pl.ds(i, 1), :]
        ranks = jnp.zeros((8, block), F32)
        for s in range(64):
            ranks += jnp.where(snap == s, wide[8 * s : 8 * s + 8], 0.0)
        for q in range(block // 32):
            rank_ref[owner_ref[i * (block // 32) + q]] = ranks[:, 32 * q : 32 * q + 32]
        total = _dot(hidden, weight_v[...]).astype(BF)
        for q in range(block // 32):
            to = pl.multiple_of(place_ref[i * (block // 32) + q] * 32, 32)
            out_ref[pl.ds(to, 32), :] = total[32 * q : 32 * q + 32]
        return carry

    lax.fori_loop(0, hid_v.shape[0] // block, body, 0)


def gather_rows(x):
    wave = jnp.concatenate([x] + [lax.ppermute(x, HID, FIRST[k]) for k in (1, 2, 3)], axis=0)
    wave = jnp.concatenate([wave] + [lax.ppermute(wave, HID, SECOND[k]) for k in (1, 2, 3)], axis=0)
    return wave, lax.ppermute(wave, HID, SIBLING)


def add_up(parts):
    total = parts[0].astype(F32)
    for part in parts[1:]:
        total = total + part.astype(F32)
    return total


def scatter_rows(x):
    n = x.shape[0]
    x = add_up([x[: n // 2], lax.ppermute(x[n // 2 :], HID, SIBLING)]).astype(BF)
    for wave in (FIRST, SECOND):
        n = x.shape[0] // 4
        parts = [x[:n]] + [
            lax.ppermute(x[k * n : (k + 1) * n], HID, wave[k]) for k in (1, 2, 3)
        ]
        x = add_up(parts)
        if wave is FIRST:
            x = x.astype(BF)
    return x


def reduce_z(parts):
    going = {}
    for step in range(4):
        for j in range(2):
            up_hops = 3 + j
            for sign, hops, perm in ((1, up_hops, UP_Z), (-1, 7 - up_hops, DOWN_Z)):
                hop = step - (4 - hops)
                if hop < 0:
                    continue
                term = parts[j][(sign * (hops - hop)) % NZ]
                if hop:
                    term = going[j, sign] + term
                going[j, sign] = lax.ppermute(term, ROWS, perm)
    return [add_up([going[j, 1], going[j, -1], parts[j][0]]) for j in range(2)]


def gather_z(x):
    half = x.shape[0] // 2
    ups, downs = [x], [x]
    for _ in range(3):
        ups.append(lax.ppermute(ups[-1], ROWS, UP_Z))
        downs.append(lax.ppermute(downs[-1], ROWS, DOWN_Z))
    far = [
        lax.ppermute(ups[3][:half], ROWS, UP_Z),
        lax.ppermute(downs[3][half:], ROWS, DOWN_Z),
    ]
    return [x] + downs[1:] + far + ups[:0:-1]


def per_device(
    tokens, snapshot, gate_weight, up_weight, down_weight, input_maps, middle_maps, down_in, down_out
):
    z, h = lax.axis_index(ROWS), lax.axis_index(HID)
    x, y, c = h // (2 * NY), h // 2 % NY, h % 2
    count = snapshot.shape[0]
    units = gate_weight.shape[1]
    width = tokens.shape[1]
    snaps = middle_maps.shape[0]

    owner = jnp.arange(32, dtype=jnp.int32)
    ox, oy, oc = owner // (2 * NY), owner // 2 % NY, owner % 2
    side = oc ^ c
    dx, dy = (x - ox) % NX, (y - oy) % NY
    arrives = side * 16 + jnp.where(oc == 0, dy * 4 + dx, dx * 4 + dy)
    ex, ey = (ox - x) % NX, (oy - y) % NY
    leaves = side * 16 + jnp.where(oc == 0, ex * 4 + ey, ey * 4 + ex)
    turned_owner = (owner + 4 * z) % 32
    leave_place = jnp.sum(
        jnp.where(turned_owner[:, None] == owner[None, :], leaves[None, :], 0), axis=1
    )
    turned = (owner - 4 * z) % 32
    at_position = (arrives[None, :] == owner[:, None])
    row_place = jnp.sum(jnp.where(at_position, turned[None, :], 0), axis=1)

    flat = snapshot[:, 0]
    index = jnp.arange(count, dtype=jnp.int32)
    same = (flat[:, None] == flat[None, :]) & (index[None, :] < index[:, None])
    slot = jnp.sum(same.astype(jnp.int32), axis=1)

    def turn(v):
        return lax.dynamic_slice_in_dim(jnp.concatenate([v, v]), z * (count // NZ), count)

    snap_turned, slot_turned = turn(flat), turn(slot)

    def by_arrival(v):
        v = v.reshape(1, 32, 32)
        return jnp.sum(jnp.where(at_position[:, :, None], v, 0), axis=1).reshape(count)

    key = by_arrival(flat * 32 + slot)
    pick = (key[None, :] == (64 * h + jnp.arange(64, dtype=jnp.int32))[:, None]).astype(BF)
    middle = (
        middle_maps.reshape(snaps // 2, 2, 2, 8, units)
        .transpose(2, 1, 0, 3, 4)
        .reshape(2, snaps * 8, units)
    )

    own, sib = gather_rows(tokens)
    down_out, own, sib = lax.optimization_barrier((down_out, own, sib))
    down_maps = lax.all_gather(down_out, HID, axis=0, tiled=True)

    ranks = pl.pallas_call(
        rank_kernel,
        out_shape=jax.ShapeDtypeStruct((NZ, 8, 128), F32),
        in_specs=[VM] * 4,
        out_specs=VM,
        compiler_params=_params(32),
        name="rank",
    )(pick, own, sib, input_maps)
    ranks = add_up(list(lax.all_to_all(ranks, ROWS, 0, 0))).astype(BF)
    ranks = lax.all_to_all(jnp.broadcast_to(ranks[None], (32, 8, 128)), HID, 0, 0)

    both = pl.pallas_call(
        up_kernel,
        out_shape=jax.ShapeDtypeStruct((2, count, units), BF),
        in_specs=[SM, VM, VM, VM, ANY, ANY, ANY, ANY, ANY],
        out_specs=VM,
        scratch_shapes=[
            pltpu.VMEM((count, width), BF),
            pltpu.VMEM((width, units), BF),
            pltpu.VMEM((width, units), BF),
            pltpu.VMEM((2, snaps * 8, units), BF),
            pltpu.SemaphoreType.DMA((3,)),
            pltpu.SemaphoreType.DMA((32,)),
        ],
        compiler_params=_params(48),
        name="gate_up",
    )(
        row_place, snap_turned[:, None], slot_turned[:, None], ranks.reshape(256, 128),
        own, sib, gate_weight, up_weight, middle,
    )
    both = both.reshape(2, NZ, count // NZ, units)
    gate, up = reduce_z([[both[j, i] for i in range(NZ)] for j in range(2)])
    hidden = (jax.nn.silu(gate) * up).astype(BF)
    pieces = gather_z(hidden)

    base, partial = pl.pallas_call(
        down_kernel,
        out_shape=(
            jax.ShapeDtypeStruct((count, width), BF),
            jax.ShapeDtypeStruct((32, 8, 32), F32),
        ),
        in_specs=[SM, SM, VM] + [ANY] * 11,
        out_specs=(VM, VM),
        scratch_shapes=[
            pltpu.VMEM((count, units), BF),
            pltpu.VMEM((units, width), BF),
            pltpu.VMEM((snaps * 8, units), BF),
            pltpu.SemaphoreType.DMA((11,)),
        ],
        compiler_params=_params(48),
        name="down",
    )(
        leave_place, turned_owner, snap_turned.reshape(4, 256),
        *pieces, down_weight, down_in.reshape(snaps * 8, units),
    )
    total = scatter_rows(base)
    down_rank = add_up(list(lax.all_to_all(partial, HID, 0, 0))).astype(BF)
    down_rank = lax.all_to_all(jnp.broadcast_to(down_rank[None], (NZ, 8, 32)), ROWS, 0, 0)
    mine = lax.dynamic_slice_in_dim(flat, h * 32, 32)
    spread = jnp.where(
        mine[None, None, :] == jnp.arange(snaps, dtype=jnp.int32)[:, None, None],
        down_rank.reshape(1, NZ * 8, 32),
        jnp.zeros((), BF),
    ).reshape(snaps * NZ * 8, 32)
    lifted = lax.dot_general(
        spread, down_maps.reshape(snaps * NZ * 8, width), (((0,), (0,)), ((), ())),
        preferred_element_type=F32,
    )
    return (total + lifted).astype(BF)


def solution(mesh):
    return jax.shard_map(
        per_device,
        mesh=mesh,
        in_specs=(
            P("hidden", "rows"),
            P(),
            P("rows", "hidden"),
            P("rows", "hidden"),
            P("hidden", "rows"),
            P("hidden", "rows", None),
            P(None, None, "rows", "hidden"),
            P(None, "rows", "hidden"),
            P("hidden", None, "rows"),
        ),
        out_specs=P("hidden", "rows"),
        check_vma=False,
    )
```

```python
import jax
import jax.numpy as jnp
from jax import lax
from jax.experimental import pallas as pl
from jax.experimental.pallas import tpu as pltpu
from jax.sharding import PartitionSpec as P

BF = jnp.bfloat16
F32 = jnp.float32
NX, NY, NZ = 4, 4, 8
ROWS, HID = "rows", "hidden"


def _h(x, y, c):
    return (x * NY + y) * 2 + c


def _plane(f):
    return [
        (_h(x, y, c), _h(*f(x, y, c))) for x in range(NX) for y in range(NY) for c in range(2)
    ]


def _on_x(k):
    return lambda x, y, c: ((x + k) % NX, y, c)


def _on_y(k):
    return lambda x, y, c: (x, (y + k) % NY, c)


FIRST = {k: _plane(lambda x, y, c, k=k: (_on_y(k) if c else _on_x(k))(x, y, c)) for k in (1, 2, 3)}
SECOND = {k: _plane(lambda x, y, c, k=k: (_on_x(k) if c else _on_y(k))(x, y, c)) for k in (1, 2, 3)}
SIBLING = _plane(lambda x, y, c: (x, y, 1 - c))
Z_MASKS = (1, 2, 7)
H_MASKS = (1, 2, 6, 8, 24)
UP_Z = [(i, (i + 1) % NZ) for i in range(NZ)]
DOWN_Z = [(i, (i - 1) % NZ) for i in range(NZ)]


def _dot(a, b):
    return jnp.dot(a, b, preferred_element_type=F32)


def _dot_nt(a, b):
    return lax.dot_general(a, b, (((1,), (1,)), ((), ())), preferred_element_type=F32)


VM = pl.BlockSpec(memory_space=pltpu.VMEM)
SM = pl.BlockSpec(memory_space=pltpu.SMEM)


def call(kernel, args, out, mib, flops, scratch=()):
    one = not isinstance(out[0][0], tuple)
    shapes = [jax.ShapeDtypeStruct(*o) for o in ([out] if one else out)]
    moved = sum(a.size * a.dtype.itemsize for a in [*args, *shapes])
    return pl.pallas_call(
        kernel,
        out_shape=shapes[0] if one else tuple(shapes),
        in_specs=[SM if a.ndim == 1 else VM for a in args],
        out_specs=VM if one else (VM,) * len(shapes),
        scratch_shapes=list(scratch),
        compiler_params=pltpu.CompilerParams(vmem_limit_bytes=mib << 20),
        cost_estimate=pl.CostEstimate(
            flops=int(flops), bytes_accessed=moved, transcendentals=0
        ),
        name=kernel.__name__,
    )(*args)


def rank_kernel(place_ref, pick_ref, own_ref, sib_ref, maps_ref, out_ref):
    half = own_ref.shape[0]
    picked = _dot(pick_ref[:, :half], own_ref[...]) + _dot(pick_ref[:, half:], sib_ref[...])
    picked = picked.astype(BF)
    cap = picked.shape[0] // 2
    ranks = jnp.concatenate(
        [_dot(picked[i * cap : (i + 1) * cap], maps_ref[i]) for i in range(2)], axis=0
    )
    turned = ranks.T
    blocks, k = out_ref.shape[0], out_ref.shape[1]
    side = blocks * k
    for r in range(blocks):
        at = slice(r * k, r * k + k)
        out_ref[place_ref[r]] = jnp.concatenate([turned[:side][at], turned[side:][at]], axis=1)


def base_kernel(place_ref, own_ref, sib_ref, gate_ref, up_ref, out_ref, rows_ref):
    for p in range(32):
        source = own_ref if p < 16 else sib_ref
        to = pl.multiple_of(place_ref[p] * 32, 32)
        rows_ref[pl.ds(to, 32), :] = source[(p % 16) * 32 : (p % 16) * 32 + 32, :]
    for j, weight_ref in enumerate((gate_ref, up_ref)):
        out_ref[j] = _dot(rows_ref[...], weight_ref[...])


def adapt_kernel(place_ref, snap_ref, slot_ref, ranks_ref, mid_ref, base_ref, out_ref):
    count = snap_ref.shape[0]
    ranks = jnp.concatenate([ranks_ref[place_ref[i]].astype(F32) for i in range(32)], axis=0)
    ranks, snap, slot = ranks.astype(BF), snap_ref[...], slot_ref[...]
    lane = lax.broadcasted_iota(jnp.int32, (count, 128), 1)
    column = lax.broadcasted_iota(jnp.int32, (1, 256), 1)
    for j in range(2):
        spread = []
        for l in range(2):
            hot = jnp.where(lane == slot + 32 * (2 * j + l), 1.0, 0.0).astype(BF)
            wide = _dot_nt(hot, ranks)
            spread.append(jnp.where(2 * (column // 8) + l == snap, wide, 0.0).astype(BF))
        total = base_ref[j] + _dot(jnp.concatenate(spread, axis=1), mid_ref[j])
        out_ref[j] = total.astype(BF)


def down_rank_kernel(place_ref, snap_ref, map_ref, *rest):
    pieces, (hid_ref, rank_ref) = rest[:9], rest[9:]
    row = 0
    for piece in pieces:
        hid_ref[row : row + piece.shape[0], :] = piece[...]
        row += piece.shape[0]
    wide = _dot_nt(map_ref[...], hid_ref[...])
    snap = snap_ref[...]
    ranks = jnp.zeros((8, snap.shape[1]), F32)
    for s in range(wide.shape[0] // 8):
        ranks += jnp.where(snap == s, wide[8 * s : 8 * s + 8], 0.0)
    rank_ref[...] = jnp.zeros_like(rank_ref)
    for i in range(32):
        rank_ref[place_ref[i], :, :32] = ranks[:, 32 * i : 32 * i + 32]


def down_kernel(place_ref, hid_ref, weight_ref, keep_ref, send_ref):
    total = _dot(hid_ref[...], weight_ref[...]).astype(BF)
    for i in range(32):
        block, to = total[32 * i : 32 * i + 32], place_ref[i]

        @pl.when(to < 16)
        def _():
            keep_ref[pl.ds(pl.multiple_of(to * 32, 32), 32), :] = block

        @pl.when(to >= 16)
        def _():
            send_ref[pl.ds(pl.multiple_of((to - 16) * 32, 32), 32), :] = block


def lift_kernel(place_ref, mine_ref, rank_ref, map_ref, out_ref):
    rows = out_ref.shape[0]
    side = rank_ref.shape[0] * rank_ref.shape[1]
    ranks = jnp.concatenate(
        [rank_ref[place_ref[i]].astype(F32) for i in range(rank_ref.shape[0])], axis=0
    )
    turned = ranks.T[:rows]
    pair = jnp.concatenate([turned, turned], axis=1)
    lane = lax.broadcasted_iota(jnp.int32, (1, 2 * side), 1) // side
    mine = mine_ref[...]
    spread = jnp.concatenate(
        [
            jnp.where(lane + 2 * m == mine, pair, 0.0).astype(BF)
            for m in range(map_ref.shape[0] // (2 * side))
        ],
        axis=1,
    )
    out_ref[...] = _dot(spread, map_ref[...])


def gather_rows(x, tables):
    wave = jnp.concatenate([x] + [lax.ppermute(x, HID, FIRST[k]) for k in (1, 2, 3)], axis=0)
    wave = jnp.concatenate([wave] + [lax.ppermute(wave, HID, SECOND[k]) for k in (1, 2, 3)], axis=0)
    wave, tables = lax.optimization_barrier((wave, tables))
    return wave, lax.ppermute(wave, HID, SIBLING), tables


def swapped(x, axis, mask):
    size = NZ if axis == ROWS else 2 * NX * NY
    return lax.ppermute(x, axis, [(i, i ^ mask) for i in range(size)])


def halve(x, axis, masks):
    for mask in masks:
        n = x.shape[0] // 2
        x = x[:n] + swapped(x[n:], axis, mask)
    return x[0]


def double(x, axis, masks):
    x = x[None]
    for mask in masks[::-1]:
        x = jnp.concatenate([x, swapped(x, axis, mask)], axis=0)
    return x


def z_place(e):
    b0, b1, b2 = e & 1, e >> 1 & 1, e >> 2
    return (b0 ^ b2) * 4 + (b1 ^ b2) * 2 + b2


def h_place(e):
    c, y0, y1, x0, x1 = (e >> i & 1 for i in range(5))
    return c * 16 + (y0 ^ y1) * 8 + y1 * 4 + (x0 ^ x1) * 2 + x1


def add_up(parts):
    total = parts[0].astype(F32)
    for part in parts[1:]:
        total = total + part.astype(F32)
    return total


def scatter_rows(keep, send):
    x = add_up([keep, lax.ppermute(send, HID, SIBLING)]).astype(BF)
    for wave in (FIRST, SECOND):
        n = x.shape[0] // 4
        parts = [x[:n]] + [
            lax.ppermute(x[k * n : (k + 1) * n], HID, wave[k]) for k in (1, 2, 3)
        ]
        if wave is FIRST:
            x = add_up(parts).astype(BF)
    return parts


def reduce_z(parts):
    going = {}
    for step in range(4):
        for j in range(2):
            up_hops = 3 + j
            for sign, hops, perm in ((1, up_hops, UP_Z), (-1, 7 - up_hops, DOWN_Z)):
                hop = step - (4 - hops)
                if hop < 0:
                    continue
                term = parts[j][(sign * (hops - hop)) % NZ]
                if hop:
                    term = going[j, sign] + term
                going[j, sign] = lax.ppermute(term, ROWS, perm)
    return [add_up([going[j, 1], going[j, -1], parts[j][0]]) for j in range(2)]


def gather_z(x):
    half = x.shape[0] // 2
    ups, downs = [x], [x]
    for _ in range(3):
        ups.append(lax.ppermute(ups[-1], ROWS, UP_Z))
        downs.append(lax.ppermute(downs[-1], ROWS, DOWN_Z))
    far = [
        lax.ppermute(ups[3][:half], ROWS, UP_Z),
        lax.ppermute(downs[3][half:], ROWS, DOWN_Z),
    ]
    return [x] + downs[1:] + far + ups[:0:-1]


def per_device(
    tokens, snapshot, gate_weight, up_weight, down_weight, input_maps, middle_maps, down_in, down_out
):
    z, h = lax.axis_index(ROWS), lax.axis_index(HID)
    x, y, c = h // (2 * NY), h // 2 % NY, h % 2
    count = snapshot.shape[0]
    units = gate_weight.shape[1]
    width = tokens.shape[1]
    snaps = middle_maps.shape[0]

    owner = jnp.arange(32, dtype=jnp.int32)
    ox, oy, oc = owner // (2 * NY), owner // 2 % NY, owner % 2
    side = oc ^ c
    dx, dy = (x - ox) % NX, (y - oy) % NY
    arrives = side * 16 + jnp.where(oc == 0, dy * 4 + dx, dx * 4 + dy)
    ex, ey = (ox - x) % NX, (oy - y) % NY
    leaves = side * 16 + jnp.where(oc == 0, ex * 4 + ey, ey * 4 + ex)
    turned_owner = (owner + 4 * z) % 32
    leave_place = jnp.sum(
        jnp.where(turned_owner[:, None] == owner[None, :], leaves[None, :], 0), axis=1
    )
    turned = (owner - 4 * z) % 32
    at_position = (arrives[None, :] == owner[:, None])
    row_place = jnp.sum(jnp.where(at_position, turned[None, :], 0), axis=1)

    flat = snapshot[:, 0]
    index = jnp.arange(count, dtype=jnp.int32)
    same = (flat[:, None] == flat[None, :]) & (index[None, :] < index[:, None])
    slot = jnp.sum(same.astype(jnp.int32), axis=1)

    def turn(v):
        return lax.dynamic_slice_in_dim(jnp.concatenate([v, v]), z * (count // NZ), count)

    snap_turned, slot_turned = turn(flat), turn(slot)

    def by_arrival(v):
        v = v.reshape(1, 32, 32)
        return jnp.sum(jnp.where(at_position[:, :, None], v, 0), axis=1).reshape(count)

    key = by_arrival(flat * 32 + slot)
    pick = (key[None, :] == (64 * h + jnp.arange(64, dtype=jnp.int32))[:, None]).astype(BF)
    middle = (
        middle_maps.reshape(snaps // 2, 2, 2, 8, units)
        .transpose(2, 1, 0, 3, 4)
        .reshape(2, snaps * 8, units)
    )

    mine = lax.dynamic_slice_in_dim(flat, h * 32, 32)
    tables = (
        pick, middle, row_place, leave_place, mine[:, None],
        z_place(jnp.arange(NZ, dtype=jnp.int32) ^ z), h_place(owner ^ h), h_place(turned_owner ^ h),
        snap_turned[:, None], slot_turned[:, None], snap_turned[None],
    )
    own, sib, tables = gather_rows(tokens, tables)
    pick, middle, row_place, leave_place, mine, by_z, by_h, by_turn, *snap_tables = tables
    snap_col, slot_col, snap_lane = snap_tables
    down_out, own, sib = lax.optimization_barrier((down_out, own, sib))
    down_maps = lax.all_gather(down_out, HID, axis=0, tiled=True)

    ranks = call(
        rank_kernel, (by_z, pick, own, sib, input_maps), ((NZ, 8, 128), F32), 12, flops=3e8
    )
    base = call(
        base_kernel, (row_place, own, sib, gate_weight, up_weight), ((2, count, units), F32), 20,
        flops=4e9, scratch=[pltpu.VMEM((count, width), BF)],
    )
    ranks = double(halve(ranks, ROWS, Z_MASKS).astype(BF), HID, H_MASKS)
    both = call(
        adapt_kernel, (by_h, snap_col, slot_col, ranks, middle, base),
        ((2, count, units), BF), 20, flops=3e9,
    )
    both = both.reshape(2, NZ, count // NZ, units)
    gate, up = reduce_z([[both[j, i] for i in range(NZ)] for j in range(2)])
    hidden = (jax.nn.silu(gate) * up).astype(BF)
    pieces = gather_z(hidden)

    hid, partial = call(
        down_rank_kernel, (by_turn, snap_lane, down_in.reshape(snaps * 8, units), *pieces),
        (((count, units), BF), ((32, 8, 128), F32)), 12, flops=1e9,
    )
    keep, send = call(
        down_kernel, (leave_place, hid, down_weight),
        (((count // 2, width), BF), ((count // 2, width), BF)), 16, flops=2e9,
    )
    parts = scatter_rows(keep, send)
    down_rank = double(halve(partial, HID, H_MASKS).astype(BF), ROWS, Z_MASKS)
    lifted = call(
        lift_kernel, (by_z, mine, down_rank, down_maps.reshape(snaps * NZ * 8, width)),
        ((32, width), F32), 8, flops=3e8,
    )
    return (add_up(parts) + lifted).astype(BF)


def solution(mesh):
    return jax.shard_map(
        per_device,
        mesh=mesh,
        in_specs=(
            P("hidden", "rows"),
            P(),
            P("rows", "hidden"),
            P("rows", "hidden"),
            P("hidden", "rows"),
            P("hidden", "rows", None),
            P(None, None, "rows", "hidden"),
            P(None, "rows", "hidden"),
            P("hidden", None, "rows"),
        ),
        out_specs=P("hidden", "rows"),
        check_vma=False,
    )
```

```python
import jax
import jax.numpy as jnp
from jax import lax
from jax.experimental import pallas as pl
from jax.experimental.pallas import tpu as pltpu
from jax.sharding import PartitionSpec as P

BF = jnp.bfloat16
F32 = jnp.float32
NX, NY, NZ = 4, 4, 8
ROWS, HID = "rows", "hidden"
CUT = 512


def _h(x, y, c):
    return (x * NY + y) * 2 + c


def _plane(f):
    return [
        (_h(x, y, c), _h(*f(x, y, c))) for x in range(NX) for y in range(NY) for c in range(2)
    ]


def _on_x(k):
    return lambda x, y, c: ((x + k) % NX, y, c)


def _on_y(k):
    return lambda x, y, c: (x, (y + k) % NY, c)


FIRST = {k: _plane(lambda x, y, c, k=k: (_on_y(k) if c else _on_x(k))(x, y, c)) for k in (1, 2, 3)}
SECOND = {k: _plane(lambda x, y, c, k=k: (_on_x(k) if c else _on_y(k))(x, y, c)) for k in (1, 2, 3)}
SIBLING = _plane(lambda x, y, c: (x, y, 1 - c))
UP_Z = [(i, (i + 1) % NZ) for i in range(NZ)]
DOWN_Z = [(i, (i - 1) % NZ) for i in range(NZ)]


def _dot(a, b):
    return jnp.dot(a, b, preferred_element_type=F32)


def _dot_nt(a, b):
    return lax.dot_general(a, b, (((1,), (1,)), ((), ())), preferred_element_type=F32)


VM = pl.BlockSpec(memory_space=pltpu.VMEM)
SM = pl.BlockSpec(memory_space=pltpu.SMEM)


def call(kernel, args, out, mib, flops, scratch=()):
    one = not isinstance(out[0][0], tuple)
    shapes = [jax.ShapeDtypeStruct(*o) for o in ([out] if one else out)]
    moved = sum(a.size * a.dtype.itemsize for a in [*args, *shapes])
    return pl.pallas_call(
        kernel,
        out_shape=shapes[0] if one else tuple(shapes),
        in_specs=[SM if a.ndim == 1 else VM for a in args],
        out_specs=VM if one else (VM,) * len(shapes),
        scratch_shapes=list(scratch),
        compiler_params=pltpu.CompilerParams(vmem_limit_bytes=mib << 20),
        cost_estimate=pl.CostEstimate(
            flops=int(flops), bytes_accessed=moved, transcendentals=0
        ),
        name=kernel.__name__,
    )(*args)


def stack_kernel(*refs):
    out_ref, row = refs[-1], 0
    for ref in refs[:-1]:
        out_ref[row : row + ref.shape[0], :] = ref[...]
        row += ref.shape[0]


def rank_kernel(pick_ref, own_ref, sib_ref, maps_ref, out_ref):
    half = own_ref.shape[0]
    picked = _dot(pick_ref[:, :half], own_ref[...]) + _dot(pick_ref[:, half:], sib_ref[...])
    picked = picked.astype(BF)
    cap = picked.shape[0] // 2
    ranks = jnp.concatenate(
        [_dot(picked[i * cap : (i + 1) * cap], maps_ref[i]) for i in range(2)], axis=0
    )
    turned = ranks.T
    blocks, k = out_ref.shape[0], out_ref.shape[1]
    side = blocks * k
    for r in range(blocks):
        at = slice(r * k, r * k + k)
        out_ref[r] = jnp.concatenate([turned[:side][at], turned[side:][at]], axis=1)


def upright(key_ref):
    key = jnp.broadcast_to(key_ref[...].astype(F32), (128, key_ref.shape[1])).T.astype(jnp.int32)
    return key // 32, key % 32


def store_blocks(refs, j, total):
    n, rows = total.shape[1], refs[0].shape[0]
    for i, ref in enumerate(refs):
        ref[:, j * n : (j + 1) * n] = total[i * rows : (i + 1) * rows].astype(BF)


def first_kernel(
    place_ref, key_ref, ranks_ref, own_ref, sib_ref, gate_ref, up_ref, mid_ref, *outs
):
    rows_ref, spread_ref, *blocks = outs
    for p in range(32):
        source = own_ref if p < 16 else sib_ref
        to = pl.multiple_of(place_ref[p] * 32, 32)
        rows_ref[pl.ds(to, 32), :] = source[(p % 16) * 32 : (p % 16) * 32 + 32, :]
    ranks = ranks_ref[...]
    snap, slot = upright(key_ref)
    snap = snap[:, :1]
    lane = lax.broadcasted_iota(jnp.int32, slot.shape, 1)
    column = lax.broadcasted_iota(jnp.int32, (1, 256), 1)
    for j, weight_ref in enumerate((gate_ref, up_ref)):
        for l in range(2):
            hot = jnp.where(lane == slot + 32 * (2 * j + l), 1.0, 0.0).astype(BF)
            wide = _dot_nt(hot, ranks)
            spread_ref[j, :, 256 * l : 256 * l + 256] = jnp.where(
                2 * (column // 8) + l == snap, wide, 0.0
            ).astype(BF)
        store_blocks(
            blocks, j,
            _dot(rows_ref[...], weight_ref[:, :CUT]) + _dot(spread_ref[j], mid_ref[j, :, :CUT]),
        )


def second_kernel(rows_ref, spread_ref, gate_ref, up_ref, mid_ref, *blocks):
    for j, weight_ref in enumerate((gate_ref, up_ref)):
        store_blocks(
            blocks, j,
            _dot(rows_ref[...], weight_ref[:, CUT:]) + _dot(spread_ref[j], mid_ref[j, :, CUT:]),
        )


def add_kernel(a_ref, b_ref, out_ref):
    out_ref[...] = (a_ref[...].astype(F32) + b_ref[...].astype(F32)).astype(BF)


def swiglu_kernel(a_ref, b_ref, c_ref, out_ref):
    total = a_ref[...].astype(F32) + b_ref[...].astype(F32) + c_ref[...].astype(F32)
    n = out_ref.shape[1]
    gate = total[:, :n]
    out_ref[...] = (gate / (1.0 + jnp.exp(-gate)) * total[:, n:]).astype(BF)


def down_kernel(place_ref, z_ref, key_ref, map_ref, weight_ref, *rest):
    pieces, (keep_ref, send_ref, hid_ref) = rest[:18], rest[18:]
    for cols, part in ((slice(0, CUT), pieces[:9]), (slice(CUT, None), pieces[9:])):
        row = 0
        for piece in part:
            hid_ref[row : row + piece.shape[0], cols] = piece[...]
            row += piece.shape[0]
    width = weight_ref.shape[1]
    hidden = hid_ref[...]
    wide = _dot_nt(hidden, map_ref[...])
    column = lax.broadcasted_iota(jnp.int32, (1, wide.shape[1]), 1)
    wide = jnp.where(column // 8 == upright(key_ref)[0][:, :1], wide, 0.0).astype(BF)
    source = lax.broadcasted_iota(jnp.int32, (wide.shape[1], 128), 0)
    lane = lax.broadcasted_iota(jnp.int32, (wide.shape[1], 128), 1)
    fold = jnp.where(lane % 64 == source % 8 + 8 * z_ref[0], 1.0, 0.0).astype(BF)
    ranks = _dot(wide, fold).astype(BF)
    total = _dot(hidden, weight_ref[...]).astype(BF)
    for i in range(32):
        at, to = slice(32 * i, 32 * i + 32), place_ref[i]

        def put(ref, to):
            rows = pl.ds(pl.multiple_of(to * 32, 32), 32)
            ref[rows, :width] = total[at]
            ref[rows, width:] = ranks[at]

        @pl.when(to < 16)
        def _():
            put(keep_ref, to)

        @pl.when(to >= 16)
        def _():
            put(send_ref, to - 16)


def sum_split_kernel(a_ref, b_ref, *outs):
    n = outs[0].shape[0]
    for k, out_ref in enumerate(outs):
        at = slice(k * n, (k + 1) * n)
        out_ref[...] = (a_ref[at, :].astype(F32) + b_ref[at, :].astype(F32)).astype(BF)


def wave_kernel(a_ref, b_ref, c_ref, d_ref, *outs):
    n = outs[0].shape[0]
    for k, out_ref in enumerate(outs):
        at = slice(k * n, (k + 1) * n)
        out_ref[...] = (
            a_ref[at, :].astype(F32) + b_ref[at, :].astype(F32)
            + c_ref[at, :].astype(F32) + d_ref[at, :].astype(F32)
        ).astype(BF)


def last_wave_kernel(a_ref, b_ref, c_ref, d_ref, out_ref, rank_ref):
    total = (
        a_ref[...].astype(F32) + b_ref[...].astype(F32)
        + c_ref[...].astype(F32) + d_ref[...].astype(F32)
    )
    width = out_ref.shape[1]
    out_ref[...] = total[:, :width]
    rank_ref[...] = total[:, width:].astype(BF)


def lift_kernel(mine_ref, total_ref, rank_ref, map_ref, out_ref):
    lane = lax.broadcasted_iota(jnp.int32, (1, 128), 1) // 64
    pair, mine = rank_ref[...].astype(F32), mine_ref[...]
    spread = jnp.concatenate(
        [
            jnp.where(lane + 2 * m == mine, pair, 0.0).astype(BF)
            for m in range(map_ref.shape[0] // 128)
        ],
        axis=1,
    )
    out_ref[...] = (total_ref[...] + _dot(spread, map_ref[...])).astype(BF)


def stack(parts):
    rows = sum(p.shape[0] for p in parts)
    return call(stack_kernel, parts, ((rows, parts[0].shape[1]), BF), 2, flops=1)


def gather_rows(x, snapshot, make_tables):
    wave = stack([x] + [lax.ppermute(x, HID, FIRST[k]) for k in (1, 2, 3)])
    wave, snapshot = lax.optimization_barrier((wave, snapshot))
    tables = make_tables(snapshot)
    pieces = [lax.ppermute(wave, HID, SECOND[k]) for k in (1, 2, 3)]
    pieces, tables = lax.optimization_barrier((pieces, tables))
    wave = stack([wave] + pieces)
    return wave, lax.ppermute(wave, HID, SIBLING), tables


def add_up(parts):
    total = parts[0].astype(F32)
    for part in parts[1:]:
        total = total + part.astype(F32)
    return total


def scatter_rows(keep, send):
    rows, width = keep.shape
    parts = call(
        sum_split_kernel, (keep, lax.ppermute(send, HID, SIBLING)),
        (((rows // 4, width), BF),) * 4, 4, flops=1,
    )
    parts = [parts[0]] + [lax.ppermute(parts[k], HID, FIRST[k]) for k in (1, 2, 3)]
    parts = call(wave_kernel, parts, (((rows // 16, width), BF),) * 4, 4, flops=1)
    return [parts[0]] + [lax.ppermute(parts[k], HID, SECOND[k]) for k in (1, 2, 3)]


def reduce_z(parts):
    going = {}
    for step in range(4):
        for g in range(2):
            up_hops = 3 + g
            for sign, hops, perm in ((-1, 7 - up_hops, DOWN_Z), (1, up_hops, UP_Z)):
                hop = step - (4 - hops)
                if hop < 0:
                    continue
                term = parts[g][(sign * (hops - hop)) % NZ]
                if hop:
                    term = call(add_kernel, (going[g, sign], term), (term.shape, BF), 2, flops=1)
                going[g, sign] = lax.ppermute(term, ROWS, perm)
    return [
        call(
            swiglu_kernel, (going[g, 1], going[g, -1], parts[g][0]),
            ((parts[g][0].shape[0], parts[g][0].shape[1] // 2), BF), 4, flops=1,
        )
        for g in range(2)
    ]


def gather_z(x):
    half = x.shape[0] // 2
    ups, downs = [x], [x]
    for _ in range(3):
        ups.append(lax.ppermute(ups[-1], ROWS, UP_Z))
        downs.append(lax.ppermute(downs[-1], ROWS, DOWN_Z))
    far = [
        lax.ppermute(ups[3][:half], ROWS, UP_Z),
        lax.ppermute(downs[3][half:], ROWS, DOWN_Z),
    ]
    return [x] + downs[1:] + far + ups[:0:-1]


def per_device(
    tokens, snapshot, gate_weight, up_weight, down_weight, input_maps, middle_maps, down_in, down_out
):
    z, h = lax.axis_index(ROWS), lax.axis_index(HID)
    x, y, c = h // (2 * NY), h // 2 % NY, h % 2
    count = snapshot.shape[0]
    units = gate_weight.shape[1]
    width = tokens.shape[1]
    snaps = middle_maps.shape[0]
    part = count // NZ

    def make_tables(inputs):
        snapshot, middle_maps = inputs
        owner = jnp.arange(32, dtype=jnp.int32)
        ox, oy, oc = owner // (2 * NY), owner // 2 % NY, owner % 2
        side = oc ^ c
        dx, dy = (x - ox) % NX, (y - oy) % NY
        arrives = side * 16 + jnp.where(oc == 0, dy * 4 + dx, dx * 4 + dy)
        ex, ey = (ox - x) % NX, (oy - y) % NY
        leaves = side * 16 + jnp.where(oc == 0, ex * 4 + ey, ey * 4 + ex)
        turned_owner = (owner + 4 * z) % 32
        leave_place = jnp.sum(
            jnp.where(turned_owner[:, None] == owner[None, :], leaves[None, :], 0), axis=1
        )
        turned = (owner - 4 * z) % 32
        at_position = arrives[None, :] == owner[:, None]
        row_place = jnp.sum(jnp.where(at_position, turned[None, :], 0), axis=1)

        flat = snapshot[:, 0]
        index = jnp.arange(count, dtype=jnp.int32)
        same = (flat[:, None] == flat[None, :]) & (index[None, :] < index[:, None])
        key = flat * 32 + jnp.sum(same.astype(jnp.int32), axis=1)
        turned_key = lax.dynamic_slice_in_dim(jnp.concatenate([key, key]), z * part, count)
        by_arrival = jnp.sum(
            jnp.where(at_position[:, :, None], key.reshape(1, 32, 32), 0), axis=1
        ).reshape(count)
        wanted = 64 * h + jnp.arange(64, dtype=jnp.int32)
        pick = (by_arrival[None, :] == wanted[:, None]).astype(BF)
        middle = (
            middle_maps.reshape(snaps // 2, 2, 2, 8, units)
            .transpose(2, 1, 0, 3, 4)
            .reshape(2, snaps * 8, units)
        )
        mine = lax.dynamic_slice_in_dim(flat, h * 32, 32)[:, None]
        return pick, middle, row_place, leave_place, mine, turned_key[None]

    own, sib, tables = gather_rows(tokens, (snapshot, middle_maps), make_tables)
    pick, middle, row_place, leave_place, mine, key = tables
    down_out, own, sib = lax.optimization_barrier((down_out, own, sib))
    down_maps = lax.all_gather(down_out, HID, axis=0, tiled=True)

    ranks = call(rank_kernel, (pick, own, sib, input_maps), ((NZ, 8, 128), F32), 4, flops=3e8)
    ranks = add_up(list(lax.all_to_all(ranks, ROWS, 0, 0))).astype(BF)
    ranks = lax.all_to_all(jnp.broadcast_to(ranks[None], (32, 8, 128)), HID, 0, 0)
    rows, spread, *early = call(
        first_kernel,
        (
            row_place, key, ranks.reshape(256, 128),
            own, sib, gate_weight, up_weight, middle,
        ),
        (((count, width), BF), ((2, count, snaps * 8), BF)) + (((part, 2 * CUT), BF),) * NZ,
        12, flops=5e9,
    )
    late = call(
        second_kernel, (rows, spread, gate_weight, up_weight, middle),
        (((part, 2 * (units - CUT)), BF),) * NZ, 10, flops=3e9,
    )
    pieces = [p for hidden in reduce_z([early, late]) for p in gather_z(hidden)]
    keep, send = call(
        down_kernel,
        (leave_place, z[None], key, down_in.reshape(snaps * 8, units), down_weight, *pieces),
        (((count // 2, width + 128), BF),) * 2, 16, flops=3e9,
        scratch=[pltpu.VMEM((count, units), BF)],
    )
    keep, send, down_maps = lax.optimization_barrier((keep, send, down_maps))
    total, rank = call(
        last_wave_kernel, scatter_rows(keep, send), (((32, width), F32), ((32, 128), BF)), 4, flops=1
    )
    for mask in (1, 2, 7):
        rank = rank + lax.ppermute(rank, ROWS, [(i, i ^ mask) for i in range(NZ)])
    return call(
        lift_kernel, (mine, total, rank, down_maps.reshape(snaps * NZ * 8, width)),
        ((32, width), BF), 4, flops=3e8,
    )


def solution(mesh):
    return jax.shard_map(
        per_device,
        mesh=mesh,
        in_specs=(
            P("hidden", "rows"),
            P(),
            P("rows", "hidden"),
            P("rows", "hidden"),
            P("hidden", "rows"),
            P("hidden", "rows", None),
            P(None, None, "rows", "hidden"),
            P(None, "rows", "hidden"),
            P("hidden", None, "rows"),
        ),
        out_specs=P("hidden", "rows"),
        check_vma=False,
    )
```

```python
import jax
import jax.numpy as jnp
from jax import lax
from jax.experimental import pallas as pl
from jax.experimental.pallas import tpu as pltpu
from jax.sharding import PartitionSpec as P

BF = jnp.bfloat16
F32 = jnp.float32
NX, NY, NZ = 4, 4, 8
ROWS, HID = "rows", "hidden"
CUT = 512


def _h(x, y, c):
    return (x * NY + y) * 2 + c


def _plane(f):
    return [
        (_h(x, y, c), _h(*f(x, y, c))) for x in range(NX) for y in range(NY) for c in range(2)
    ]


def _on_x(k):
    return lambda x, y, c: ((x + k) % NX, y, c)


def _on_y(k):
    return lambda x, y, c: (x, (y + k) % NY, c)


FIRST = {k: _plane(lambda x, y, c, k=k: (_on_y(k) if c else _on_x(k))(x, y, c)) for k in (1, 2, 3)}
SECOND = {k: _plane(lambda x, y, c, k=k: (_on_x(k) if c else _on_y(k))(x, y, c)) for k in (1, 2, 3)}
SIBLING = _plane(lambda x, y, c: (x, y, 1 - c))
UP_Z = [(i, (i + 1) % NZ) for i in range(NZ)]
DOWN_Z = [(i, (i - 1) % NZ) for i in range(NZ)]


def _dot(a, b):
    return jnp.dot(a, b, preferred_element_type=F32)


def _dot_nt(a, b):
    return lax.dot_general(a, b, (((1,), (1,)), ((), ())), preferred_element_type=F32)


VM = pl.BlockSpec(memory_space=pltpu.VMEM)
SM = pl.BlockSpec(memory_space=pltpu.SMEM)


def call(kernel, args, out, mib, flops, scratch=()):
    one = not isinstance(out[0][0], tuple)
    shapes = [jax.ShapeDtypeStruct(*o) for o in ([out] if one else out)]
    moved = sum(a.size * a.dtype.itemsize for a in [*args, *shapes])
    return pl.pallas_call(
        kernel,
        out_shape=shapes[0] if one else tuple(shapes),
        in_specs=[SM if a.ndim == 1 else VM for a in args],
        out_specs=VM if one else (VM,) * len(shapes),
        scratch_shapes=list(scratch),
        compiler_params=pltpu.CompilerParams(vmem_limit_bytes=mib << 20),
        cost_estimate=pl.CostEstimate(
            flops=int(flops), bytes_accessed=moved, transcendentals=0
        ),
        name=kernel.__name__,
    )(*args)


def stack_kernel(*refs):
    out_ref, row = refs[-1], 0
    for ref in refs[:-1]:
        out_ref[row : row + ref.shape[0], :] = ref[...]
        row += ref.shape[0]


def rank_kernel(pick_ref, own_ref, sib_ref, maps_ref, out_ref):
    half = own_ref.shape[0]
    picked = _dot(pick_ref[:, :half], own_ref[...]) + _dot(pick_ref[:, half:], sib_ref[...])
    picked = picked.astype(BF)
    cap = picked.shape[0] // 2
    ranks = jnp.concatenate(
        [_dot(picked[i * cap : (i + 1) * cap], maps_ref[i]) for i in range(2)], axis=0
    )
    turned = ranks.T
    blocks, k = out_ref.shape[0], out_ref.shape[1]
    side = blocks * k
    for r in range(blocks):
        at = slice(r * k, r * k + k)
        out_ref[r] = jnp.concatenate([turned[:side][at], turned[side:][at]], axis=1)


def upright(key_ref):
    key = jnp.broadcast_to(key_ref[...].astype(F32), (128, key_ref.shape[1])).T.astype(jnp.int32)
    return key // 32, key % 32


def store_blocks(refs, j, total):
    n, rows = total.shape[1], refs[0].shape[0]
    for i, ref in enumerate(refs):
        ref[:, j * n : (j + 1) * n] = total[i * rows : (i + 1) * rows].astype(BF)


def first_kernel(
    place_ref, key_ref, ranks_ref, own_ref, sib_ref, gate_ref, up_ref, mid_ref, *outs
):
    rows_ref, spread_ref, *blocks = outs
    for p in range(32):
        source = own_ref if p < 16 else sib_ref
        to = pl.multiple_of(place_ref[p] * 32, 32)
        rows_ref[pl.ds(to, 32), :] = source[(p % 16) * 32 : (p % 16) * 32 + 32, :]
    ranks = ranks_ref[...]
    snap, slot = upright(key_ref)
    snap = snap[:, :1]
    lane = lax.broadcasted_iota(jnp.int32, slot.shape, 1)
    column = lax.broadcasted_iota(jnp.int32, (1, 256), 1)
    for j, weight_ref in enumerate((gate_ref, up_ref)):
        for l in range(2):
            hot = jnp.where(lane == slot + 32 * (2 * j + l), 1.0, 0.0).astype(BF)
            wide = _dot_nt(hot, ranks)
            spread_ref[j, :, 256 * l : 256 * l + 256] = jnp.where(
                2 * (column // 8) + l == snap, wide, 0.0
            ).astype(BF)
        store_blocks(
            blocks, j,
            _dot(rows_ref[...], weight_ref[:, :CUT]) + _dot(spread_ref[j], mid_ref[j, :, :CUT]),
        )


def second_kernel(at_ref, key_ref, rows_ref, spread_ref, gate_ref, up_ref, mid_ref, *outs):
    mine_ref, *blocks, snap_ref = outs
    snap_ref[...] = upright(key_ref)[0]
    mine_ref[...] = snap_ref[pl.ds(pl.multiple_of(at_ref[2] * 32, 32), 32), :]
    for j, weight_ref in enumerate((gate_ref, up_ref)):
        store_blocks(
            blocks, j,
            _dot(rows_ref[...], weight_ref[:, CUT:]) + _dot(spread_ref[j], mid_ref[j, :, CUT:]),
        )


def add_kernel(a_ref, b_ref, out_ref):
    out_ref[...] = (a_ref[...].astype(F32) + b_ref[...].astype(F32)).astype(BF)


def swiglu_kernel(a_ref, b_ref, c_ref, out_ref):
    total = a_ref[...].astype(F32) + b_ref[...].astype(F32) + c_ref[...].astype(F32)
    n = out_ref.shape[1]
    gate = total[:, :n]
    out_ref[...] = (gate / (1.0 + jnp.exp(-gate)) * total[:, n:]).astype(BF)


def down_rows(at_ref, place_ref, key_ref, map_ref, weight_ref, hid_ref, out_ref, odd):
    snap = upright(key_ref)[0][:, :1]
    blocks = range(place_ref.shape[0] // 2)
    snap = [
        jnp.concatenate([snap[64 * i + 32 * p : 64 * i + 32 * p + 32] for i in blocks])
        for p in range(2)
    ]
    hidden = hid_ref[odd]
    wide = _dot_nt(hidden, map_ref[...])
    column = lax.broadcasted_iota(jnp.int32, (1, wide.shape[1]), 1)
    wide = jnp.where(column // 8 == jnp.where(odd == 1, snap[1], snap[0]), wide, 0.0).astype(BF)
    source = lax.broadcasted_iota(jnp.int32, (wide.shape[1], 128), 0)
    lane = lax.broadcasted_iota(jnp.int32, (wide.shape[1], 128), 1)
    fold = jnp.where(lane % 64 == source % 8 + 8 * at_ref[0], 1.0, 0.0).astype(BF)
    ranks = _dot(wide, fold).astype(BF)
    total = _dot(hidden, weight_ref[...]).astype(BF)
    width = total.shape[1]
    for i in blocks:
        rows = pl.ds(pl.multiple_of((place_ref[2 * i + odd] & 15) * 32, 32), 32)
        out_ref[rows, :width] = total[32 * i : 32 * i + 32]
        out_ref[rows, width:] = ranks[32 * i : 32 * i + 32]


def down_send_kernel(at_ref, place_ref, key_ref, map_ref, weight_ref, *rest):
    pieces, (out_ref, hid_ref) = rest[:16], rest[16:]
    for cols, part in ((slice(0, CUT), pieces[:8]), (slice(CUT, None), pieces[8:])):
        for m, piece in enumerate(part):
            for q in range(4):
                to = 32 * (2 * m + q // 2)
                hid_ref[q % 2, to : to + 32, cols] = piece[32 * q : 32 * q + 32, :]
    down_rows(at_ref, place_ref, key_ref, map_ref, weight_ref, hid_ref, out_ref, 1 - at_ref[1])


def down_keep_kernel(at_ref, place_ref, key_ref, map_ref, weight_ref, hid_ref, out_ref):
    down_rows(at_ref, place_ref, key_ref, map_ref, weight_ref, hid_ref, out_ref, at_ref[1])


def sum_split_kernel(a_ref, b_ref, *outs):
    n = outs[0].shape[0]
    for k, out_ref in enumerate(outs):
        at = slice(k * n, (k + 1) * n)
        out_ref[...] = (a_ref[at, :].astype(F32) + b_ref[at, :].astype(F32)).astype(BF)


def wave_kernel(a_ref, b_ref, c_ref, d_ref, *outs):
    n = outs[0].shape[0]
    for k, out_ref in enumerate(outs):
        at = slice(k * n, (k + 1) * n)
        out_ref[...] = (
            a_ref[at, :].astype(F32) + b_ref[at, :].astype(F32)
            + c_ref[at, :].astype(F32) + d_ref[at, :].astype(F32)
        ).astype(BF)


def last_wave_kernel(maps_ref, a_ref, b_ref, c_ref, d_ref, out_ref, rank_ref):
    del maps_ref
    total = (
        a_ref[...].astype(F32) + b_ref[...].astype(F32)
        + c_ref[...].astype(F32) + d_ref[...].astype(F32)
    )
    width = out_ref.shape[1]
    out_ref[...] = total[:, :width]
    rank_ref[...] = total[:, width:].astype(BF)


def lift_kernel(mine_ref, total_ref, rank_ref, map_ref, out_ref):
    lane = lax.broadcasted_iota(jnp.int32, mine_ref.shape, 1) // 64
    pair, mine = jnp.sum(rank_ref[...].astype(F32), axis=0), mine_ref[...]
    spread = jnp.concatenate(
        [
            jnp.where(lane + 2 * m == mine, pair, 0.0).astype(BF)
            for m in range(map_ref.shape[0] // 128)
        ],
        axis=1,
    )
    out_ref[...] = (total_ref[...] + _dot(spread, map_ref[...])).astype(BF)


def stack(parts):
    rows = sum(p.shape[0] for p in parts)
    return call(stack_kernel, parts, ((rows, parts[0].shape[1]), BF), 2, flops=1)


def gather_rows(x, inputs, make_tables):
    wave = stack([x] + [lax.ppermute(x, HID, FIRST[k]) for k in (1, 2, 3)])
    wave, inputs = lax.optimization_barrier((wave, inputs))
    tables = make_tables(*inputs)
    wave = stack([wave] + [lax.ppermute(wave, HID, SECOND[k]) for k in (1, 2, 3)])
    wave, tables = lax.optimization_barrier((wave, tables))
    return wave, lax.ppermute(wave, HID, SIBLING), tables


def add_up(parts):
    total = parts[0].astype(F32)
    for part in parts[1:]:
        total = total + part.astype(F32)
    return total


def scatter_rows(keep, send):
    rows, width = keep.shape
    parts = call(
        sum_split_kernel, (keep, lax.ppermute(send, HID, SIBLING)),
        (((rows // 4, width), BF),) * 4, 4, flops=1,
    )
    parts = [parts[0]] + [lax.ppermute(parts[k], HID, FIRST[k]) for k in (1, 2, 3)]
    parts = call(wave_kernel, parts, (((rows // 16, width), BF),) * 4, 4, flops=1)
    return [parts[0]] + [lax.ppermute(parts[k], HID, SECOND[k]) for k in (1, 2, 3)]


def reduce_z(parts):
    going = {}
    for step in range(4):
        for g in range(2):
            up_hops = 3 + g
            for sign, hops, perm in ((-1, 7 - up_hops, DOWN_Z), (1, up_hops, UP_Z)):
                hop = step - (4 - hops)
                if hop < 0:
                    continue
                term = parts[g][(sign * (hops - hop)) % NZ]
                if hop:
                    term = call(add_kernel, (going[g, sign], term), (term.shape, BF), 2, flops=1)
                going[g, sign] = lax.ppermute(term, ROWS, perm)
    return [
        call(
            swiglu_kernel, (going[g, 1], going[g, -1], parts[g][0]),
            ((parts[g][0].shape[0], parts[g][0].shape[1] // 2), BF), 4, flops=1,
        )
        for g in range(2)
    ]


def gather_z(x, far_up):
    ups, downs = [x], [x]
    for hop in range(4):
        if hop < 3 or far_up:
            ups.append(lax.ppermute(ups[-1], ROWS, UP_Z))
        if hop < 3 or not far_up:
            downs.append(lax.ppermute(downs[-1], ROWS, DOWN_Z))
    return downs + ups[:0:-1]


def per_device(
    tokens, snapshot, gate_weight, up_weight, down_weight, input_maps, middle_maps, down_in, down_out
):
    count = snapshot.shape[0]
    units = gate_weight.shape[1]
    width = tokens.shape[1]
    snaps = middle_maps.shape[0]
    part = count // NZ

    def make_tables(snapshot, middle_maps, z, h):
        x, y, c = h // (2 * NY), h // 2 % NY, h % 2
        owner = jnp.arange(32, dtype=jnp.int32)
        ox, oy, oc = owner // (2 * NY), owner // 2 % NY, owner % 2
        side = oc ^ c
        dx, dy = (x - ox) % NX, (y - oy) % NY
        arrives = side * 16 + jnp.where(oc == 0, dy * 4 + dx, dx * 4 + dy)
        ex, ey = (ox - x) % NX, (oy - y) % NY
        leaves = side * 16 + jnp.where(oc == 0, ex * 4 + ey, ey * 4 + ex)
        turned_owner = (owner + 4 * z) % 32
        leave_place = jnp.sum(
            jnp.where(turned_owner[:, None] == owner[None, :], leaves[None, :], 0), axis=1
        )
        turned = (owner - 4 * z) % 32
        at_position = arrives[None, :] == owner[:, None]
        row_place = jnp.sum(jnp.where(at_position, turned[None, :], 0), axis=1)

        flat = snapshot[:, 0]
        index = jnp.arange(count, dtype=jnp.int32)
        same = (flat[:, None] == flat[None, :]) & (index[None, :] < index[:, None])
        key = flat * 32 + jnp.sum(same.astype(jnp.int32), axis=1)
        turned_key = lax.dynamic_slice_in_dim(jnp.concatenate([key, key]), z * part, count)
        by_arrival = jnp.sum(
            jnp.where(at_position[:, :, None], key.reshape(1, 32, 32), 0), axis=1
        ).reshape(count)
        wanted = 64 * h + jnp.arange(64, dtype=jnp.int32)
        pick = (by_arrival[None, :] == wanted[:, None]).astype(BF)
        middle = (
            middle_maps.reshape(snaps // 2, 2, 2, 8, units)
            .transpose(2, 1, 0, 3, 4)
            .reshape(2, snaps * 8, units)
        )
        at = jnp.stack([z, c, (h - 4 * z) % 32])
        return pick, middle, row_place, leave_place, turned_key[None], at

    own, sib, (pick, middle, row_place, leave_place, key, at) = gather_rows(
        tokens, (snapshot, middle_maps, lax.axis_index(ROWS), lax.axis_index(HID)), make_tables
    )
    ranks = call(rank_kernel, (pick, own, sib, input_maps), ((NZ, 8, 128), F32), 4, flops=3e8)
    ranks, down_out = lax.optimization_barrier((ranks, down_out))
    down_maps = lax.all_gather(down_out, HID, axis=0, tiled=True)
    ranks = add_up(list(lax.all_to_all(ranks, ROWS, 0, 0))).astype(BF)
    ranks = lax.all_to_all(jnp.broadcast_to(ranks[None], (32, 8, 128)), HID, 0, 0)
    rows, spread, *early = call(
        first_kernel,
        (
            row_place, key, ranks.reshape(256, 128),
            own, sib, gate_weight, up_weight, middle,
        ),
        (((count, width), BF), ((2, count, snaps * 8), BF)) + (((part, 2 * CUT), BF),) * NZ,
        12, flops=5e9,
    )
    mine, *late = call(
        second_kernel, (at, key, rows, spread, gate_weight, up_weight, middle),
        (((32, 128), jnp.int32),) + (((part, 2 * (units - CUT)), BF),) * NZ, 10, flops=3e9,
        scratch=[pltpu.VMEM((count, 128), jnp.int32)],
    )
    pieces = [
        p for g, hidden in enumerate(reduce_z([early, late])) for p in gather_z(hidden, g == 0)
    ]
    down_in = down_in.reshape(snaps * 8, units)
    half = ((count // 2, width + 128), BF)
    send, hid = call(
        down_send_kernel, (at, leave_place, key, down_in, down_weight, *pieces),
        (half, ((2, count // 2, units), BF)), 10, flops=2e9,
    )
    send, down_maps = lax.optimization_barrier((send, down_maps))
    keep = call(
        down_keep_kernel, (at, leave_place, key, down_in, down_weight, hid), half, 10, flops=2e9
    )
    maps = down_maps.reshape(snaps * NZ * 8, width)
    total, rank = call(
        last_wave_kernel, (maps, *scatter_rows(keep, send)), (((32, width), F32), ((32, 128), BF)),
        4, flops=1,
    )
    rank, total = lax.optimization_barrier((rank, total))
    rank = lax.all_to_all(jnp.broadcast_to(rank[None], (NZ, 32, 128)), ROWS, 0, 0)
    return call(lift_kernel, (mine, total, rank, maps), ((32, width), BF), 4, flops=3e8)


def solution(mesh):
    return jax.shard_map(
        per_device,
        mesh=mesh,
        in_specs=(
            P("hidden", "rows"),
            P(),
            P("rows", "hidden"),
            P("rows", "hidden"),
            P("hidden", "rows"),
            P("hidden", "rows", None),
            P(None, None, "rows", "hidden"),
            P(None, "rows", "hidden"),
            P("hidden", None, "rows"),
        ),
        out_specs=P("hidden", "rows"),
        check_vma=False,
    )
```

```python
import functools

import jax
import jax.numpy as jnp
from jax import lax
from jax.experimental import pallas as pl
from jax.experimental.pallas import tpu as pltpu
from jax.sharding import PartitionSpec as P

BF = jnp.bfloat16
F32 = jnp.float32
NX, NY, NZ = 4, 4, 8
ROWS, HID = "rows", "hidden"
BLOCK = 256
WAIT = 4e9
CUT = 512


def _h(x, y, c):
    return (x * NY + y) * 2 + c


def _plane(f):
    return [
        (_h(x, y, c), _h(*f(x, y, c))) for x in range(NX) for y in range(NY) for c in range(2)
    ]


def _on_x(k):
    return lambda x, y, c: ((x + k) % NX, y, c)


def _on_y(k):
    return lambda x, y, c: (x, (y + k) % NY, c)


FIRST = {k: _plane(lambda x, y, c, k=k: (_on_y(k) if c else _on_x(k))(x, y, c)) for k in (1, 2, 3)}
SECOND = {k: _plane(lambda x, y, c, k=k: (_on_x(k) if c else _on_y(k))(x, y, c)) for k in (1, 2, 3)}
SIBLING = _plane(lambda x, y, c: (x, y, 1 - c))
UP_Z = [(i, (i + 1) % NZ) for i in range(NZ)]
DOWN_Z = [(i, (i - 1) % NZ) for i in range(NZ)]


def _dot(a, b):
    return jnp.dot(a, b, preferred_element_type=F32)


def _dot_nt(a, b):
    return lax.dot_general(a, b, (((1,), (1,)), ((), ())), preferred_element_type=F32)


VM = pl.BlockSpec(memory_space=pltpu.VMEM)
ANY = pl.BlockSpec(memory_space=pl.ANY)
SM = pl.BlockSpec(memory_space=pltpu.SMEM)


def call(kernel, args, out, mib, flops, scratch=(), far=()):
    one = not isinstance(out[0][0], tuple)
    shapes = [jax.ShapeDtypeStruct(*o) for o in ([out] if one else out)]
    moved = sum(a.size * a.dtype.itemsize for a in [*args, *shapes])
    return pl.pallas_call(
        kernel,
        out_shape=shapes[0] if one else tuple(shapes),
        in_specs=[SM if a.ndim == 1 else ANY if i in far else VM for i, a in enumerate(args)],
        out_specs=VM if one else (VM,) * len(shapes),
        scratch_shapes=list(scratch),
        compiler_params=pltpu.CompilerParams(vmem_limit_bytes=mib << 20),
        cost_estimate=pl.CostEstimate(
            flops=int(flops), bytes_accessed=moved, transcendentals=0
        ),
        name=getattr(kernel, "func", kernel).__name__,
    )(*args)


def place():
    z, h = lax.axis_index(ROWS), lax.axis_index(HID)
    return z, h >> 3, h >> 1 & 3, h & 1


def arrived_from(p):
    z, x, y, c = place()
    core = c ^ (p >> 4)
    far, near = p >> 2 & 3, p & 3
    ox, oy = (x - jnp.where(core == 0, near, far)) & 3, (y - jnp.where(core == 0, far, near)) & 3
    return (ox * 8 + oy * 2 + core - 4 * z) & 31


def leaves_to(i):
    z, x, y, _ = place()
    h = (i + 4 * z) & 31
    ex, ey = ((h >> 3) - x) & 3, ((h >> 1 & 3) - y) & 3
    return jnp.where(h & 1 == 0, ex * 4 + ey, ey * 4 + ex)


def key_kernel(snap_ref, out_ref, key_ref):
    n = snap_ref.shape[0]
    earlier = lax.broadcasted_iota(jnp.int32, (128, 128), 0) < lax.broadcasted_iota(
        jnp.int32, (128, 128), 1
    )
    columns = [
        jnp.broadcast_to(snap_ref[r : r + 1, :].astype(F32), (128, 128)).T.astype(jnp.int32)
        for r in range(n)
    ]
    for r in range(n):
        row = snap_ref[r : r + 1, :]
        count = jnp.where((columns[r] == row) & earlier, 1, 0)
        for q in range(r):
            count += jnp.where(columns[q] == row, 1, 0)
        key_ref[r : r + 1, :] = row * 32 + jnp.sum(count, axis=0, keepdims=True)
    z = lax.axis_index(ROWS)
    for i in range(n):
        out_ref[i : i + 1, :] = key_ref[pl.ds((z + i) & (n - 1), 1), :]


def stack_kernel(*refs):
    *ins, out_ref, sems = refs
    copies, row = [], 0
    for i, ref in enumerate(ins):
        to = out_ref.at[pl.ds(row, ref.shape[0])]
        copies.append(pltpu.make_async_copy(ref, to, sems.at[i]))
        row += ref.shape[0]
    for copy in copies:
        copy.start()
    for copy in copies:
        copy.wait()


def rank_kernel(
    key_ref, own_ref, sib_ref, maps_ref, out_ref, rows_ref, sems
):
    copies = []
    for p in range(32):
        source = own_ref if p < 16 else sib_ref
        to = pl.multiple_of(arrived_from(p) * 32, 32)
        copies.append(
            pltpu.make_async_copy(
                source.at[pl.ds(p % 16 * 32, 32)], rows_ref.at[pl.ds(to, 32)], sems.at[p]
            )
        )
        copies[-1].start()
    wanted = 64 * lax.axis_index(HID) + lax.broadcasted_iota(jnp.int32, (64, 128), 0)
    pick = jnp.concatenate(
        [
            jnp.where(key_ref[i : i + 1, :] == wanted, 1.0, 0.0).astype(BF)
            for i in range(key_ref.shape[0])
        ],
        axis=1,
    )
    for copy in copies:
        copy.wait()
    picked = _dot(pick, rows_ref[...]).astype(BF)
    cap = picked.shape[0] // 2
    ranks = jnp.concatenate(
        [_dot(picked[i * cap : (i + 1) * cap], maps_ref[i]) for i in range(2)], axis=0
    )
    turned = ranks.T
    blocks, k = out_ref.shape[0], out_ref.shape[1]
    side = blocks * k
    for r in range(blocks):
        at = slice(r * k, r * k + k)
        out_ref[r] = jnp.concatenate([turned[:side][at], turned[side:][at]], axis=1)


def upright(key_ref, snap_ref, slot_ref=None):
    n = key_ref.shape[1]
    for i in range(key_ref.shape[0]):
        key = jnp.broadcast_to(key_ref[i : i + 1, :].astype(F32), (n, n)).T.astype(jnp.int32)
        snap_ref[i * n : (i + 1) * n, :] = key >> 5
        if slot_ref is not None:
            slot_ref[i * n : (i + 1) * n, :] = key & 31


def in_blocks(count, rows, body):
    lax.fori_loop(
        0, count // rows, lambda i, _: body(pl.ds(pl.multiple_of(i * rows, rows), rows)) or 0, 0
    )


def send_copies(all_ref, up_ref, down_ref, up_hops):
    rows = up_ref.shape[0]
    for ref, i in ((up_ref, up_hops), (down_ref, 1 + up_hops)):
        ref[...] = all_ref[i * rows : (i + 1) * rows, :]


def first_kernel(
    key_ref, ranks_ref, rows_ref, gate_ref, up_ref, mid_ref,
    spread_ref, all_ref, go_up_ref, go_down_ref, snap_ref, slot_ref,
):
    upright(key_ref, snap_ref, slot_ref)
    column = lax.broadcasted_iota(jnp.int32, (1, 256), 1)

    def body(at):
        snap, slot = snap_ref[at, :1], slot_ref[at, :]
        lane = lax.broadcasted_iota(jnp.int32, slot.shape, 1)
        for j, weight_ref in enumerate((gate_ref, up_ref)):
            spread = []
            for l in range(2):
                hot = jnp.where(lane == slot + 32 * (2 * j + l), 1.0, 0.0).astype(BF)
                wide = _dot_nt(hot, ranks_ref[...])
                spread.append(jnp.where(2 * (column // 8) + l == snap, wide, 0.0).astype(BF))
            spread = jnp.concatenate(spread, axis=1)
            spread_ref[j, at, :] = spread
            total = _dot(rows_ref[at, :], weight_ref[:, :CUT]) + _dot(spread, mid_ref[j, :, :CUT])
            all_ref[at, j * CUT : (j + 1) * CUT] = total.astype(BF)

    in_blocks(rows_ref.shape[0], BLOCK, body)
    send_copies(all_ref, go_up_ref, go_down_ref, 3)


def second_kernel(
    key_ref, rows_ref, spread_ref, gate_ref, up_ref, mid_ref,
    mine_ref, all_ref, go_up_ref, go_down_ref, snap_ref,
):
    upright(key_ref, snap_ref)
    block = (lax.axis_index(HID) - 4 * lax.axis_index(ROWS)) & 31
    mine_ref[...] = snap_ref[pl.ds(pl.multiple_of(block * 32, 32), 32), :]
    n = all_ref.shape[1] // 2

    def body(at):
        for j, weight_ref in enumerate((gate_ref, up_ref)):
            total = _dot(rows_ref[at, :], weight_ref[:, CUT:])
            total += _dot(spread_ref[j, at, :], mid_ref[j, :, CUT:])
            all_ref[at, j * n : (j + 1) * n] = total.astype(BF)

    in_blocks(rows_ref.shape[0], BLOCK, body)
    send_copies(all_ref, go_up_ref, go_down_ref, 4)


def strip(i, rows):
    return pl.ds(pl.multiple_of(i * rows, rows), rows)


def add_kernel(i, a_ref, all_ref, out_ref):
    n = out_ref.shape[0] // 16

    def body(r, _):
        at = strip(r, 16)
        own = all_ref[strip(i * n + r, 16), :]
        out_ref[at, :] = (a_ref[at, :].astype(F32) + own.astype(F32)).astype(BF)
        return 0

    lax.fori_loop(0, n, body, 0)


def swiglu_kernel(a_ref, b_ref, all_ref, out_ref):
    n = out_ref.shape[1]

    def body(r, _):
        at = strip(r, 16)
        total = a_ref[at, :].astype(F32) + b_ref[at, :].astype(F32) + all_ref[at, :].astype(F32)
        gate = total[:, :n]
        out_ref[at, :] = (gate / (1.0 + jnp.exp(-gate)) * total[:, n:]).astype(BF)
        return 0

    lax.fori_loop(0, out_ref.shape[0] // 16, body, 0)


def down_rows(key_ref, map_ref, weight_ref, hid_ref, out_ref, snap_ref, odd):
    upright(key_ref, snap_ref)
    rank, width = map_ref.shape[0], weight_ref.shape[1]
    column = lax.broadcasted_iota(jnp.int32, (1, rank), 1)
    source = lax.broadcasted_iota(jnp.int32, (rank, 128), 0)
    lane = lax.broadcasted_iota(jnp.int32, (rank, 128), 1)
    fold = jnp.where(lane % 64 == source % 8 + 8 * lax.axis_index(ROWS), 1.0, 0.0).astype(BF)
    group = BLOCK // 32

    def body(i, _):
        at = strip(i, BLOCK)
        hidden = hid_ref[at, :] if len(hid_ref.shape) == 2 else hid_ref[odd, at, :]
        blocks = [2 * (group * i + q) + odd for q in range(group)]
        snap = jnp.concatenate(
            [snap_ref[pl.ds(pl.multiple_of(32 * b, 32), 32), :] for b in blocks], axis=0
        )[:, :1]
        wide = jnp.where(column // 8 == snap, _dot_nt(hidden, map_ref[...]), 0.0).astype(BF)
        ranks = _dot(wide, fold).astype(BF)
        total = _dot(hidden, weight_ref[...]).astype(BF)
        for q, b in enumerate(blocks):
            rows = pl.ds(pl.multiple_of(leaves_to(b) * 32, 32), 32)
            out_ref[rows, :width] = total[32 * q : 32 * q + 32]
            out_ref[rows, width:] = ranks[32 * q : 32 * q + 32]
        return 0

    lax.fori_loop(0, out_ref.shape[0] // BLOCK, body, 0)


def down_send_kernel(key_ref, map_ref, weight_ref, *rest):
    pieces, (out_ref, keep_ref, snap_ref, hid_ref) = rest[:16], rest[16:]
    for cols, part in ((slice(0, CUT), pieces[:8]), (slice(CUT, None), pieces[8:])):
        for m, piece in enumerate(part):
            for q in range(4):
                to = 32 * (2 * m + q // 2)
                hid_ref[q % 2, to : to + 32, cols] = piece[32 * q : 32 * q + 32, :]
    core = lax.axis_index(HID) & 1
    keep_ref[...] = hid_ref[core]
    down_rows(key_ref, map_ref, weight_ref, hid_ref, out_ref, snap_ref, 1 - core)


def down_keep_kernel(key_ref, map_ref, weight_ref, hid_ref, out_ref, snap_ref):
    core = lax.axis_index(HID) & 1
    down_rows(key_ref, map_ref, weight_ref, hid_ref, out_ref, snap_ref, core)


def sum_kernel(count, *refs):
    ins, outs = refs[:count], refs[count:]
    n = outs[0].shape[0] // 16
    for k, out_ref in enumerate(outs):

        def body(r, _):
            at = strip(k * n + r, 16)
            out_ref[strip(r, 16), :] = sum(ref[at, :].astype(F32) for ref in ins).astype(BF)
            return 0

        lax.fori_loop(0, n, body, 0)


def last_wave_kernel(a_ref, b_ref, c_ref, d_ref, out_ref, rank_ref):
    total = (
        a_ref[...].astype(F32) + b_ref[...].astype(F32)
        + c_ref[...].astype(F32) + d_ref[...].astype(F32)
    )
    width = out_ref.shape[1]
    out_ref[...] = total[:, :width]
    rank_ref[...] = total[:, width:].astype(BF)


def lift_kernel(mine_ref, total_ref, rank_ref, map_ref, out_ref):
    lane = lax.broadcasted_iota(jnp.int32, mine_ref.shape, 1) // 64
    pair, mine = jnp.sum(rank_ref[...].astype(F32), axis=0), mine_ref[...]
    spread = jnp.concatenate(
        [
            jnp.where(lane + 2 * m == mine, pair, 0.0).astype(BF)
            for m in range(map_ref.shape[0] // 128)
        ],
        axis=1,
    )
    out_ref[...] = (total_ref[...] + _dot(spread, map_ref[...])).astype(BF)


def stack(parts):
    rows = sum(p.shape[0] for p in parts)
    return call(
        stack_kernel, parts, ((rows, parts[0].shape[1]), BF), 2, flops=1,
        scratch=[pltpu.SemaphoreType.DMA((len(parts),))], far=range(len(parts)),
    )


def gather_rows(x, later):
    wave = stack([x] + [lax.ppermute(x, HID, FIRST[k]) for k in (1, 2, 3)])
    wave, later = lax.optimization_barrier((wave, later))
    wave = stack([wave] + [lax.ppermute(wave, HID, SECOND[k]) for k in (1, 2, 3)])
    return wave, later


def add_up(parts):
    total = parts[0].astype(F32)
    for part in parts[1:]:
        total = total + part.astype(F32)
    return total


def scatter_rows(keep, send):
    rows, width = keep.shape
    parts = call(
        functools.partial(sum_kernel, 2), (keep, lax.ppermute(send, HID, SIBLING)),
        (((rows // 4, width), BF),) * 4, 4, flops=WAIT,
    )
    parts = [parts[0]] + [lax.ppermute(parts[k], HID, FIRST[k]) for k in (1, 2, 3)]
    parts = call(
        functools.partial(sum_kernel, 4), parts, (((rows // 16, width), BF),) * 4, 4, flops=WAIT
    )
    return [parts[0]] + [lax.ppermute(parts[k], HID, SECOND[k]) for k in (1, 2, 3)]


def reduce_z(streams):
    going = {}
    for step in range(4):
        for g, (terms, go_up, go_down) in enumerate(streams):
            up_hops, shape = 3 + g, go_up.shape
            for sign, hops, perm in ((-1, 7 - up_hops, DOWN_Z), (1, up_hops, UP_Z)):
                hop = step - (4 - hops)
                if hop < 0:
                    continue
                term = go_up if sign == 1 else go_down
                if hop:
                    add = functools.partial(add_kernel, (sign * (hops - hop)) % NZ)
                    term = call(add, (going[g, sign], terms), (shape, BF), 2, flops=1)
                going[g, sign] = lax.ppermute(term, ROWS, perm)
    return [
        call(
            swiglu_kernel, (going[g, 1], going[g, -1], terms),
            ((go_up.shape[0], go_up.shape[1] // 2), BF), 4, flops=1,
        )
        for g, (terms, go_up, _) in enumerate(streams)
    ]


def gather_z(x, far_up):
    ups, downs = [x], [x]
    for hop in range(4):
        if hop < 3 or far_up:
            ups.append(lax.ppermute(ups[-1], ROWS, UP_Z))
        if hop < 3 or not far_up:
            downs.append(lax.ppermute(downs[-1], ROWS, DOWN_Z))
    return downs + ups[:0:-1]


def per_device(
    tokens, snapshot, gate_weight, up_weight, down_weight, input_maps, middle_maps, down_in, down_out
):
    count = snapshot.shape[0]
    units = gate_weight.shape[1]
    width = tokens.shape[1]
    snaps = middle_maps.shape[0]
    part = count // NZ

    own, (snapshot, middle_maps) = gather_rows(tokens, (snapshot, middle_maps))
    key = call(
        key_kernel, (snapshot.reshape(NZ, part),), ((NZ, part), jnp.int32), 2, flops=1,
        scratch=[pltpu.VMEM((NZ, part), jnp.int32)],
    )
    middle = (
        middle_maps.reshape(snaps // 2, 2, 2, 8, units)
        .transpose(2, 1, 0, 3, 4)
        .reshape(2, snaps * 8, units)
    )
    own, key, middle, down_out = lax.optimization_barrier((own, key, middle, down_out))
    sib = lax.ppermute(own, HID, SIBLING)
    down_maps = lax.all_gather(down_out, HID, axis=0, tiled=True)
    ranks, rows = call(
        rank_kernel, (key, own, sib, input_maps),
        (((NZ, 8, 128), F32), ((count, width), BF)), 5, flops=3e8,
        scratch=[pltpu.SemaphoreType.DMA((32,))], far=(1, 2),
    )
    ranks = add_up(list(lax.all_to_all(ranks, ROWS, 0, 0))).astype(BF)
    ranks = lax.all_to_all(jnp.broadcast_to(ranks[None], (32, 8, 128)), HID, 0, 0)
    def stream(n):
        return ((count, 2 * n), BF), ((part, 2 * n), BF), ((part, 2 * n), BF)

    marks = pltpu.VMEM((count, 128), jnp.int32)
    spread, *early = call(
        first_kernel, (key, ranks.reshape(256, 128), rows, gate_weight, up_weight, middle),
        (((2, count, snaps * 8), BF), *stream(CUT)), 12, flops=5e9, scratch=[marks, marks],
    )
    mine, *late = call(
        second_kernel, (key, rows, spread, gate_weight, up_weight, middle),
        (((32, 128), jnp.int32), *stream(units - CUT)), 10, flops=3e9, scratch=[marks],
    )
    pieces = [
        p for g, hidden in enumerate(reduce_z([early, late])) for p in gather_z(hidden, g == 0)
    ]
    down_in = down_in.reshape(snaps * 8, units)
    half = ((count // 2, width + 128), BF)
    send, hid = call(
        down_send_kernel, (key, down_in, down_weight, *pieces),
        (half, ((count // 2, units), BF)), 10, flops=2e9,
        scratch=[marks, pltpu.VMEM((2, count // 2, units), BF)],
    )
    keep = call(
        down_keep_kernel, (key, down_in, down_weight, hid), half, 10, flops=2e9,
        scratch=[marks],
    )
    keep, down_maps = lax.optimization_barrier((keep, down_maps))
    maps = down_maps.reshape(snaps * NZ * 8, width)
    total, rank = call(
        last_wave_kernel, scatter_rows(keep, send), (((32, width), F32), ((32, 128), BF)),
        4, flops=WAIT,
    )
    rank, total = lax.optimization_barrier((rank, total))
    rank = lax.all_to_all(jnp.broadcast_to(rank[None], (NZ, 32, 128)), ROWS, 0, 0)
    return call(lift_kernel, (mine, total, rank, maps), ((32, width), BF), 4, flops=3e8)


def solution(mesh):
    return jax.shard_map(
        per_device,
        mesh=mesh,
        in_specs=(
            P("hidden", "rows"),
            P(),
            P("rows", "hidden"),
            P("rows", "hidden"),
            P("hidden", "rows"),
            P("hidden", "rows", None),
            P(None, None, "rows", "hidden"),
            P(None, "rows", "hidden"),
            P("hidden", None, "rows"),
        ),
        out_specs=P("hidden", "rows"),
        check_vma=False,
    )
```

```python
import functools

import jax
import jax.numpy as jnp
from jax import lax
from jax.experimental import pallas as pl
from jax.experimental.pallas import tpu as pltpu
from jax.sharding import PartitionSpec as P

BF = jnp.bfloat16
F32 = jnp.float32
NX, NY, NZ = 4, 4, 8
ROWS, HID = "rows", "hidden"
BLOCK = 512
WAIT = 4e9
CUT = 512


def _h(x, y, c):
    return (x * NY + y) * 2 + c


def _plane(f):
    return [
        (_h(x, y, c), _h(*f(x, y, c))) for x in range(NX) for y in range(NY) for c in range(2)
    ]


def _on_x(k):
    return lambda x, y, c: ((x + k) % NX, y, c)


def _on_y(k):
    return lambda x, y, c: (x, (y + k) % NY, c)


FIRST = {k: _plane(lambda x, y, c, k=k: (_on_y(k) if c else _on_x(k))(x, y, c)) for k in (1, 2, 3)}
SECOND = {k: _plane(lambda x, y, c, k=k: (_on_x(k) if c else _on_y(k))(x, y, c)) for k in (1, 2, 3)}
SIBLING = _plane(lambda x, y, c: (x, y, 1 - c))
UP_Z = [(i, (i + 1) % NZ) for i in range(NZ)]
DOWN_Z = [(i, (i - 1) % NZ) for i in range(NZ)]


def _dot(a, b):
    return jnp.dot(a, b, preferred_element_type=F32)


def _dot_nt(a, b):
    return lax.dot_general(a, b, (((1,), (1,)), ((), ())), preferred_element_type=F32)


VM = pl.BlockSpec(memory_space=pltpu.VMEM)
ANY = pl.BlockSpec(memory_space=pl.ANY)
SM = pl.BlockSpec(memory_space=pltpu.SMEM)


def call(kernel, args, out, mib, flops, scratch=(), far=()):
    one = not isinstance(out[0][0], tuple)
    shapes = [jax.ShapeDtypeStruct(*o) for o in ([out] if one else out)]
    moved = sum(a.size * a.dtype.itemsize for a in [*args, *shapes])
    return pl.pallas_call(
        kernel,
        out_shape=shapes[0] if one else tuple(shapes),
        in_specs=[SM if a.ndim == 1 else ANY if i in far else VM for i, a in enumerate(args)],
        out_specs=VM if one else (VM,) * len(shapes),
        scratch_shapes=list(scratch),
        compiler_params=pltpu.CompilerParams(vmem_limit_bytes=mib << 20),
        cost_estimate=pl.CostEstimate(
            flops=int(flops), bytes_accessed=moved, transcendentals=0
        ),
        name=getattr(kernel, "func", kernel).__name__,
    )(*args)


def place():
    z, h = lax.axis_index(ROWS), lax.axis_index(HID)
    return z, h >> 3, h >> 1 & 3, h & 1


def arrived_from(p):
    z, x, y, c = place()
    core = c ^ (p >> 4)
    far, near = p >> 2 & 3, p & 3
    ox, oy = (x - jnp.where(core == 0, near, far)) & 3, (y - jnp.where(core == 0, far, near)) & 3
    return (ox * 8 + oy * 2 + core - 4 * z) & 31


def leaves_to(i):
    z, x, y, _ = place()
    h = (i + 4 * z) & 31
    ex, ey = ((h >> 3) - x) & 3, ((h >> 1 & 3) - y) & 3
    return jnp.where(h & 1 == 0, ex * 4 + ey, ey * 4 + ex)


def key_kernel(snap_ref, out_ref, key_ref):
    n = snap_ref.shape[0]
    earlier = lax.broadcasted_iota(jnp.int32, (128, 128), 0) < lax.broadcasted_iota(
        jnp.int32, (128, 128), 1
    )
    columns = [
        jnp.broadcast_to(snap_ref[r : r + 1, :].astype(F32), (128, 128)).T.astype(jnp.int32)
        for r in range(n)
    ]
    for r in range(n):
        row = snap_ref[r : r + 1, :]
        count = jnp.where((columns[r] == row) & earlier, 1, 0)
        for q in range(r):
            count += jnp.where(columns[q] == row, 1, 0)
        key_ref[r : r + 1, :] = row * 32 + jnp.sum(count, axis=0, keepdims=True)
    z = lax.axis_index(ROWS)
    for i in range(n):
        out_ref[i : i + 1, :] = key_ref[pl.ds((z + i) & (n - 1), 1), :]


def stack_kernel(*refs):
    *ins, out_ref, sems = refs
    copies, row = [], 0
    for i, ref in enumerate(ins):
        to = out_ref.at[pl.ds(row, ref.shape[0])]
        copies.append(pltpu.make_async_copy(ref, to, sems.at[i]))
        row += ref.shape[0]
    for copy in copies:
        copy.start()
    for copy in copies:
        copy.wait()


def rank_kernel(key_ref, own_ref, sib_ref, maps_ref, out_ref, rows_ref):
    for p in range(32):
        source = own_ref if p < 16 else sib_ref
        to = pl.multiple_of(arrived_from(p) * 32, 32)
        rows_ref[pl.ds(to, 32), :] = source[p % 16 * 32 : p % 16 * 32 + 32, :]
    wanted = 64 * lax.axis_index(HID) + lax.broadcasted_iota(jnp.int32, (64, 128), 0)
    pick = jnp.concatenate(
        [
            jnp.where(key_ref[i : i + 1, :] == wanted, 1.0, 0.0).astype(BF)
            for i in range(key_ref.shape[0])
        ],
        axis=1,
    )
    picked = _dot(pick, rows_ref[...]).astype(BF)
    cap = picked.shape[0] // 2
    ranks = jnp.concatenate(
        [_dot(picked[i * cap : (i + 1) * cap], maps_ref[i]) for i in range(2)], axis=0
    )
    turned = ranks.T
    blocks, k = out_ref.shape[0], out_ref.shape[1]
    side = blocks * k
    for r in range(blocks):
        at = slice(r * k, r * k + k)
        out_ref[r] = jnp.concatenate([turned[:side][at], turned[side:][at]], axis=1)


def upright(key_ref, snap_ref, slot_ref=None):
    n = key_ref.shape[1]
    for i in range(key_ref.shape[0]):
        key = jnp.broadcast_to(key_ref[i : i + 1, :].astype(F32), (n, n)).T.astype(jnp.int32)
        snap_ref[i * n : (i + 1) * n, :] = key >> 5
        if slot_ref is not None:
            slot_ref[i * n : (i + 1) * n, :] = key & 31


def in_blocks(count, rows, body):
    lax.fori_loop(
        0, count // rows, lambda i, _: body(pl.ds(pl.multiple_of(i * rows, rows), rows)) or 0, 0
    )


def send_copies(all_ref, up_ref, down_ref, up_hops):
    rows = up_ref.shape[0]
    for ref, i in ((up_ref, up_hops), (down_ref, 1 + up_hops)):
        ref[...] = all_ref[i * rows : (i + 1) * rows, :]


def first_kernel(
    key_ref, ranks_ref, rows_ref, gate_ref, up_ref, mid_ref,
    spread_ref, all_ref, go_up_ref, go_down_ref, snap_ref, slot_ref,
):
    upright(key_ref, snap_ref, slot_ref)
    column = lax.broadcasted_iota(jnp.int32, (1, 256), 1)

    def body(at):
        snap, slot = snap_ref[at, :1], slot_ref[at, :]
        lane = lax.broadcasted_iota(jnp.int32, slot.shape, 1)
        for j, weight_ref in enumerate((gate_ref, up_ref)):
            spread = []
            for l in range(2):
                hot = jnp.where(lane == slot + 32 * (2 * j + l), 1.0, 0.0).astype(BF)
                wide = _dot_nt(hot, ranks_ref[...])
                spread.append(jnp.where(2 * (column // 8) + l == snap, wide, 0.0).astype(BF))
            spread = jnp.concatenate(spread, axis=1)
            spread_ref[j, at, :] = spread
            total = _dot(rows_ref[at, :], weight_ref[:, :CUT]) + _dot(spread, mid_ref[j, :, :CUT])
            all_ref[at, j * CUT : (j + 1) * CUT] = total.astype(BF)

    in_blocks(rows_ref.shape[0], BLOCK, body)
    send_copies(all_ref, go_up_ref, go_down_ref, 3)


def second_kernel(
    key_ref, rows_ref, spread_ref, gate_ref, up_ref, mid_ref,
    mine_ref, all_ref, go_up_ref, go_down_ref, snap_ref,
):
    upright(key_ref, snap_ref)
    block = (lax.axis_index(HID) - 4 * lax.axis_index(ROWS)) & 31
    mine_ref[...] = snap_ref[pl.ds(pl.multiple_of(block * 32, 32), 32), :]
    n = all_ref.shape[1] // 2

    def body(at):
        for j, weight_ref in enumerate((gate_ref, up_ref)):
            total = _dot(rows_ref[at, :], weight_ref[:, CUT:])
            total += _dot(spread_ref[j, at, :], mid_ref[j, :, CUT:])
            all_ref[at, j * n : (j + 1) * n] = total.astype(BF)

    in_blocks(rows_ref.shape[0], BLOCK, body)
    send_copies(all_ref, go_up_ref, go_down_ref, 4)


def strip(i, rows):
    return pl.ds(pl.multiple_of(i * rows, rows), rows)


def add_kernel(i, a_ref, all_ref, out_ref):
    n = out_ref.shape[0] // 16

    def body(r, _):
        at = strip(r, 16)
        own = all_ref[strip(i * n + r, 16), :]
        out_ref[at, :] = (a_ref[at, :].astype(F32) + own.astype(F32)).astype(BF)
        return 0

    lax.fori_loop(0, n, body, 0)


def swiglu_kernel(a_ref, b_ref, all_ref, out_ref):
    n = out_ref.shape[1]

    def body(r, _):
        at = strip(r, 16)
        total = a_ref[at, :].astype(F32) + b_ref[at, :].astype(F32) + all_ref[at, :].astype(F32)
        gate = total[:, :n]
        out_ref[at, :] = (gate / (1.0 + jnp.exp(-gate)) * total[:, n:]).astype(BF)
        return 0

    lax.fori_loop(0, out_ref.shape[0] // 16, body, 0)


def down_rows(key_ref, map_ref, weight_ref, hid_ref, out_ref, snap_ref, odd):
    upright(key_ref, snap_ref)
    rank, width = map_ref.shape[0], weight_ref.shape[1]
    column = lax.broadcasted_iota(jnp.int32, (1, rank), 1)
    source = lax.broadcasted_iota(jnp.int32, (rank, 128), 0)
    lane = lax.broadcasted_iota(jnp.int32, (rank, 128), 1)
    fold = jnp.where(lane % 64 == source % 8 + 8 * lax.axis_index(ROWS), 1.0, 0.0).astype(BF)
    group = BLOCK // 32

    def body(i, _):
        at = strip(i, BLOCK)
        hidden = hid_ref[at, :] if len(hid_ref.shape) == 2 else hid_ref[odd, at, :]
        blocks = [2 * (group * i + q) + odd for q in range(group)]
        snap = jnp.concatenate(
            [snap_ref[pl.ds(pl.multiple_of(32 * b, 32), 32), :] for b in blocks], axis=0
        )[:, :1]
        wide = jnp.where(column // 8 == snap, _dot_nt(hidden, map_ref[...]), 0.0).astype(BF)
        ranks = _dot(wide, fold).astype(BF)
        total = _dot(hidden, weight_ref[...]).astype(BF)
        for q, b in enumerate(blocks):
            rows = pl.ds(pl.multiple_of(leaves_to(b) * 32, 32), 32)
            out_ref[rows, :width] = total[32 * q : 32 * q + 32]
            out_ref[rows, width:] = ranks[32 * q : 32 * q + 32]
        return 0

    lax.fori_loop(0, out_ref.shape[0] // BLOCK, body, 0)


def down_send_kernel(key_ref, map_ref, weight_ref, *rest):
    pieces, (out_ref, keep_ref, snap_ref, hid_ref) = rest[:16], rest[16:]
    for cols, part in ((slice(0, CUT), pieces[:8]), (slice(CUT, None), pieces[8:])):
        for m, piece in enumerate(part):
            for q in range(4):
                to = 32 * (2 * m + q // 2)
                hid_ref[q % 2, to : to + 32, cols] = piece[32 * q : 32 * q + 32, :]
    core = lax.axis_index(HID) & 1
    keep_ref[...] = hid_ref[core]
    down_rows(key_ref, map_ref, weight_ref, hid_ref, out_ref, snap_ref, 1 - core)


def down_keep_kernel(key_ref, map_ref, weight_ref, hid_ref, out_ref, snap_ref):
    core = lax.axis_index(HID) & 1
    down_rows(key_ref, map_ref, weight_ref, hid_ref, out_ref, snap_ref, core)


def sum_kernel(count, *refs):
    ins, outs = refs[:count], refs[count:]
    n = outs[0].shape[0] // 16
    for k, out_ref in enumerate(outs):

        def body(r, _):
            at = strip(k * n + r, 16)
            out_ref[strip(r, 16), :] = sum(ref[at, :].astype(F32) for ref in ins).astype(BF)
            return 0

        lax.fori_loop(0, n, body, 0)


def last_wave_kernel(a_ref, b_ref, c_ref, d_ref, out_ref, rank_ref):
    total = (
        a_ref[...].astype(F32) + b_ref[...].astype(F32)
        + c_ref[...].astype(F32) + d_ref[...].astype(F32)
    )
    width = out_ref.shape[1]
    out_ref[...] = total[:, :width]
    rank_ref[...] = total[:, width:].astype(BF)


def lift_kernel(mine_ref, total_ref, rank_ref, map_ref, out_ref):
    lane = lax.broadcasted_iota(jnp.int32, mine_ref.shape, 1) // 64
    pair, mine = jnp.sum(rank_ref[...].astype(F32), axis=0), mine_ref[...]
    spread = jnp.concatenate(
        [
            jnp.where(lane + 2 * m == mine, pair, 0.0).astype(BF)
            for m in range(map_ref.shape[0] // 128)
        ],
        axis=1,
    )
    out_ref[...] = (total_ref[...] + _dot(spread, map_ref[...])).astype(BF)


def stack(parts):
    rows = sum(p.shape[0] for p in parts)
    return call(
        stack_kernel, parts, ((rows, parts[0].shape[1]), BF), 2, flops=1,
        scratch=[pltpu.SemaphoreType.DMA((len(parts),))], far=range(len(parts)),
    )


def gather_rows(x, later):
    wave = stack([x] + [lax.ppermute(x, HID, FIRST[k]) for k in (1, 2, 3)])
    wave, later = lax.optimization_barrier((wave, later))
    wave = stack([wave] + [lax.ppermute(wave, HID, SECOND[k]) for k in (1, 2, 3)])
    return wave, later


def add_up(parts):
    total = parts[0].astype(F32)
    for part in parts[1:]:
        total = total + part.astype(F32)
    return total


def scatter_rows(keep, send):
    rows, width = keep.shape
    parts = call(
        functools.partial(sum_kernel, 2), (keep, lax.ppermute(send, HID, SIBLING)),
        (((rows // 4, width), BF),) * 4, 4, flops=WAIT,
    )
    parts = [parts[0]] + [lax.ppermute(parts[k], HID, FIRST[k]) for k in (1, 2, 3)]
    parts = call(
        functools.partial(sum_kernel, 4), parts, (((rows // 16, width), BF),) * 4, 4, flops=WAIT
    )
    return [parts[0]] + [lax.ppermute(parts[k], HID, SECOND[k]) for k in (1, 2, 3)]


def reduce_z(streams):
    going = {}
    for step in range(4):
        for g in range(2):
            if (step, g) == (0, 1):
                going[0, -1], streams[1] = lax.optimization_barrier((going[0, -1], streams[1]))
            terms, go_up, go_down = streams[g]
            up_hops, shape = 3 + g, go_up.shape
            for sign, hops, perm in ((-1, 7 - up_hops, DOWN_Z), (1, up_hops, UP_Z)):
                hop = step - (4 - hops)
                if hop < 0:
                    continue
                term = go_up if sign == 1 else go_down
                if hop:
                    add = functools.partial(add_kernel, (sign * (hops - hop)) % NZ)
                    term = call(add, (going[g, sign], terms), (shape, BF), 2, flops=1)
                going[g, sign] = lax.ppermute(term, ROWS, perm)
    return [
        call(
            swiglu_kernel, (going[g, 1], going[g, -1], terms),
            ((go_up.shape[0], go_up.shape[1] // 2), BF), 4, flops=1,
        )
        for g, (terms, go_up, _) in enumerate(streams)
    ]


def gather_z(x, far_up):
    ups, downs = [x], [x]
    for hop in range(4):
        if hop < 3 or far_up:
            ups.append(lax.ppermute(ups[-1], ROWS, UP_Z))
        if hop < 3 or not far_up:
            downs.append(lax.ppermute(downs[-1], ROWS, DOWN_Z))
    return downs + ups[:0:-1]


def per_device(
    tokens, snapshot, gate_weight, up_weight, down_weight, input_maps, middle_maps, down_in, down_out
):
    count = snapshot.shape[0]
    units = gate_weight.shape[1]
    width = tokens.shape[1]
    snaps = middle_maps.shape[0]
    part = count // NZ

    own, (snapshot, middle_maps) = gather_rows(tokens, (snapshot, middle_maps))
    key = call(
        key_kernel, (snapshot.reshape(NZ, part),), ((NZ, part), jnp.int32), 2, flops=1,
        scratch=[pltpu.VMEM((NZ, part), jnp.int32)],
    )
    middle = (
        middle_maps.reshape(snaps // 2, 2, 2, 8, units)
        .transpose(2, 1, 0, 3, 4)
        .reshape(2, snaps * 8, units)
    )
    own, key, middle, down_out = lax.optimization_barrier((own, key, middle, down_out))
    sib = lax.ppermute(own, HID, SIBLING)
    down_maps = lax.all_gather(down_out, HID, axis=0, tiled=True)
    ranks, rows = call(
        rank_kernel, (key, own, sib, input_maps),
        (((NZ, 8, 128), F32), ((count, width), BF)), 5, flops=3e8,
    )
    ranks = add_up(list(lax.all_to_all(ranks, ROWS, 0, 0))).astype(BF)
    ranks = lax.all_to_all(jnp.broadcast_to(ranks[None], (32, 8, 128)), HID, 0, 0)
    def stream(n):
        return ((count, 2 * n), BF), ((part, 2 * n), BF), ((part, 2 * n), BF)

    marks = pltpu.VMEM((count, 128), jnp.int32)
    spread, *early = call(
        first_kernel, (key, ranks.reshape(256, 128), rows, gate_weight, up_weight, middle),
        (((2, count, snaps * 8), BF), *stream(CUT)), 12, flops=5e9, scratch=[marks, marks],
    )
    mine, *late = call(
        second_kernel, (key, rows, spread, gate_weight, up_weight, middle),
        (((32, 128), jnp.int32), *stream(units - CUT)), 10, flops=3e9, scratch=[marks],
    )
    pieces = [
        p for g, hidden in enumerate(reduce_z([early, late])) for p in gather_z(hidden, g == 0)
    ]
    down_in = down_in.reshape(snaps * 8, units)
    half = ((count // 2, width + 128), BF)
    send, hid = call(
        down_send_kernel, (key, down_in, down_weight, *pieces),
        (half, ((count // 2, units), BF)), 10, flops=2e9,
        scratch=[marks, pltpu.VMEM((2, count // 2, units), BF)],
    )
    keep = call(
        down_keep_kernel, (key, down_in, down_weight, hid), half, 10, flops=2e9,
        scratch=[marks],
    )
    total, rank = call(
        last_wave_kernel, scatter_rows(keep, send), (((32, width), F32), ((32, 128), BF)),
        4, flops=WAIT,
    )
    rank, total, down_maps = lax.optimization_barrier((rank, total, down_maps))
    maps = down_maps.reshape(snaps * NZ * 8, width)
    rank = lax.all_to_all(jnp.broadcast_to(rank[None], (NZ, 32, 128)), ROWS, 0, 0)
    return call(lift_kernel, (mine, total, rank, maps), ((32, width), BF), 4, flops=3e8)


def solution(mesh):
    return jax.shard_map(
        per_device,
        mesh=mesh,
        in_specs=(
            P("hidden", "rows"),
            P(),
            P("rows", "hidden"),
            P("rows", "hidden"),
            P("hidden", "rows"),
            P("hidden", "rows", None),
            P(None, None, "rows", "hidden"),
            P(None, "rows", "hidden"),
            P("hidden", None, "rows"),
        ),
        out_specs=P("hidden", "rows"),
        check_vma=False,
    )
```

```python
import functools

import jax
import jax.numpy as jnp
from jax import lax
from jax.experimental import pallas as pl
from jax.experimental.pallas import tpu as pltpu
from jax.sharding import PartitionSpec as P

BF = jnp.bfloat16
F32 = jnp.float32
NX, NY, NZ = 4, 4, 8
ROWS, HID = "rows", "hidden"
BLOCK = 256
WAIT = 4e9
CUT = 512


def _h(x, y, c):
    return (x * NY + y) * 2 + c


def _plane(f):
    return [
        (_h(x, y, c), _h(*f(x, y, c))) for x in range(NX) for y in range(NY) for c in range(2)
    ]


def _on_x(k):
    return lambda x, y, c: ((x + k) % NX, y, c)


def _on_y(k):
    return lambda x, y, c: (x, (y + k) % NY, c)


FIRST = {k: _plane(lambda x, y, c, k=k: (_on_y(k) if c else _on_x(k))(x, y, c)) for k in (1, 2, 3)}
SECOND = {k: _plane(lambda x, y, c, k=k: (_on_x(k) if c else _on_y(k))(x, y, c)) for k in (1, 2, 3)}
SIBLING = _plane(lambda x, y, c: (x, y, 1 - c))
UP_Z = [(i, (i + 1) % NZ) for i in range(NZ)]
DOWN_Z = [(i, (i - 1) % NZ) for i in range(NZ)]


def _dot(a, b):
    return jnp.dot(a, b, preferred_element_type=F32)


def _dot_nt(a, b):
    return lax.dot_general(a, b, (((1,), (1,)), ((), ())), preferred_element_type=F32)


VM = pl.BlockSpec(memory_space=pltpu.VMEM)
ANY = pl.BlockSpec(memory_space=pl.ANY)
SM = pl.BlockSpec(memory_space=pltpu.SMEM)


def call(kernel, args, out, mib, flops, scratch=(), far=()):
    one = not isinstance(out[0][0], tuple)
    shapes = [jax.ShapeDtypeStruct(*o) for o in ([out] if one else out)]
    moved = sum(a.size * a.dtype.itemsize for a in [*args, *shapes])
    return pl.pallas_call(
        kernel,
        out_shape=shapes[0] if one else tuple(shapes),
        in_specs=[SM if a.ndim == 1 else ANY if i in far else VM for i, a in enumerate(args)],
        out_specs=VM if one else (VM,) * len(shapes),
        scratch_shapes=list(scratch),
        compiler_params=pltpu.CompilerParams(vmem_limit_bytes=mib << 20),
        cost_estimate=pl.CostEstimate(
            flops=int(flops), bytes_accessed=moved, transcendentals=0
        ),
        name=getattr(kernel, "func", kernel).__name__,
    )(*args)


def place():
    z, h = lax.axis_index(ROWS), lax.axis_index(HID)
    return z, h >> 3, h >> 1 & 3, h & 1


def arrived_from(p):
    z, x, y, c = place()
    core = c ^ (p >> 4)
    far, near = p >> 2 & 3, p & 3
    ox, oy = (x - jnp.where(core == 0, near, far)) & 3, (y - jnp.where(core == 0, far, near)) & 3
    return (ox * 8 + oy * 2 + core - 4 * z) & 31


def leaves_to(i):
    z, x, y, _ = place()
    h = (i + 4 * z) & 31
    ex, ey = ((h >> 3) - x) & 3, ((h >> 1 & 3) - y) & 3
    return jnp.where(h & 1 == 0, ex * 4 + ey, ey * 4 + ex)


def key_kernel(snap_ref, out_ref, key_ref):
    n = snap_ref.shape[0]
    earlier = lax.broadcasted_iota(jnp.int32, (128, 128), 0) < lax.broadcasted_iota(
        jnp.int32, (128, 128), 1
    )
    columns = [
        jnp.broadcast_to(snap_ref[r : r + 1, :].astype(F32), (128, 128)).T.astype(jnp.int32)
        for r in range(n)
    ]
    for r in range(n):
        row = snap_ref[r : r + 1, :]
        count = jnp.where((columns[r] == row) & earlier, 1, 0)
        for q in range(r):
            count += jnp.where(columns[q] == row, 1, 0)
        key_ref[r : r + 1, :] = row * 32 + jnp.sum(count, axis=0, keepdims=True)
    z = lax.axis_index(ROWS)
    for i in range(n):
        out_ref[i : i + 1, :] = key_ref[pl.ds((z + i) & (n - 1), 1), :]


def stack_kernel(*refs):
    *ins, out_ref, sems = refs
    copies, row = [], 0
    for i, ref in enumerate(ins):
        to = out_ref.at[pl.ds(row, ref.shape[0])]
        copies.append(pltpu.make_async_copy(ref, to, sems.at[i]))
        row += ref.shape[0]
    for copy in copies:
        copy.start()
    for copy in copies:
        copy.wait()


def rank_kernel(key_ref, own_ref, sib_ref, maps_ref, out_ref, rows_ref):
    for side, source in enumerate((own_ref, sib_ref)):

        def move(p, _):
            to = strip(arrived_from(16 * side + p), 32)
            rows_ref[to, :] = source[strip(p, 32), :]
            return 0

        lax.fori_loop(0, 16, move, 0)
    wanted = 64 * lax.axis_index(HID) + lax.broadcasted_iota(jnp.int32, (64, 128), 0)
    pick = jnp.concatenate(
        [
            jnp.where(key_ref[i : i + 1, :] == wanted, 1.0, 0.0).astype(BF)
            for i in range(key_ref.shape[0])
        ],
        axis=1,
    )
    picked = _dot(pick, rows_ref[...]).astype(BF)
    cap = picked.shape[0] // 2
    ranks = jnp.concatenate(
        [_dot(picked[i * cap : (i + 1) * cap], maps_ref[i]) for i in range(2)], axis=0
    )
    turned = ranks.T
    blocks, k = out_ref.shape[0], out_ref.shape[1]
    side = blocks * k
    for r in range(blocks):
        at = slice(r * k, r * k + k)
        out_ref[r] = jnp.concatenate([turned[:side][at], turned[side:][at]], axis=1)


def upright(key_ref, snap_ref, slot_ref=None):
    n = key_ref.shape[1]
    for i in range(key_ref.shape[0]):
        key = jnp.broadcast_to(key_ref[i : i + 1, :].astype(F32), (n, n)).T.astype(jnp.int32)
        snap_ref[i * n : (i + 1) * n, :] = key >> 5
        if slot_ref is not None:
            slot_ref[i * n : (i + 1) * n, :] = key & 31


def in_blocks(count, rows, body):
    lax.fori_loop(
        0, count // rows, lambda i, _: body(pl.ds(pl.multiple_of(i * rows, rows), rows)) or 0, 0
    )


def send_copies(all_ref, up_ref, down_ref, up_hops):
    rows = up_ref.shape[0]
    for ref, i in ((up_ref, up_hops), (down_ref, 1 + up_hops)):
        ref[...] = all_ref[i * rows : (i + 1) * rows, :]


def first_kernel(
    key_ref, ranks_ref, rows_ref, gate_ref, up_ref, mid_ref,
    spread_ref, all_ref, go_up_ref, go_down_ref, snap_ref, slot_ref,
):
    upright(key_ref, snap_ref, slot_ref)
    column = lax.broadcasted_iota(jnp.int32, (1, 256), 1)

    def body(at):
        snap, slot = snap_ref[at, :1], slot_ref[at, :]
        lane = lax.broadcasted_iota(jnp.int32, slot.shape, 1)
        for j, weight_ref in enumerate((gate_ref, up_ref)):
            spread = []
            for l in range(2):
                hot = jnp.where(lane == slot + 32 * (2 * j + l), 1.0, 0.0).astype(BF)
                wide = _dot_nt(hot, ranks_ref[...])
                spread.append(jnp.where(2 * (column // 8) + l == snap, wide, 0.0).astype(BF))
            spread = jnp.concatenate(spread, axis=1)
            spread_ref[j, at, :] = spread
            total = _dot(rows_ref[at, :], weight_ref[:, :CUT]) + _dot(spread, mid_ref[j, :, :CUT])
            all_ref[at, j * CUT : (j + 1) * CUT] = total.astype(BF)

    in_blocks(rows_ref.shape[0], BLOCK, body)
    send_copies(all_ref, go_up_ref, go_down_ref, 3)


def second_kernel(
    key_ref, rows_ref, spread_ref, gate_ref, up_ref, mid_ref,
    mine_ref, all_ref, go_up_ref, go_down_ref, snap_ref,
):
    upright(key_ref, snap_ref)
    block = (lax.axis_index(HID) - 4 * lax.axis_index(ROWS)) & 31
    mine_ref[...] = snap_ref[pl.ds(pl.multiple_of(block * 32, 32), 32), :]
    n = all_ref.shape[1] // 2

    def body(at):
        for j, weight_ref in enumerate((gate_ref, up_ref)):
            total = _dot(rows_ref[at, :], weight_ref[:, CUT:])
            total += _dot(spread_ref[j, at, :], mid_ref[j, :, CUT:])
            all_ref[at, j * n : (j + 1) * n] = total.astype(BF)

    in_blocks(rows_ref.shape[0], BLOCK, body)
    send_copies(all_ref, go_up_ref, go_down_ref, 4)


def strip(i, rows):
    return pl.ds(pl.multiple_of(i * rows, rows), rows)


def add_kernel(i, a_ref, all_ref, out_ref):
    n = out_ref.shape[0] // 16

    def body(r, _):
        at = strip(r, 16)
        own = all_ref[strip(i * n + r, 16), :]
        out_ref[at, :] = (a_ref[at, :].astype(F32) + own.astype(F32)).astype(BF)
        return 0

    lax.fori_loop(0, n, body, 0)


def swiglu_kernel(a_ref, b_ref, all_ref, out_ref):
    n = out_ref.shape[1]

    def body(r, _):
        at = strip(r, 16)
        total = a_ref[at, :].astype(F32) + b_ref[at, :].astype(F32) + all_ref[at, :].astype(F32)
        gate = total[:, :n]
        out_ref[at, :] = (gate / (1.0 + jnp.exp(-gate)) * total[:, n:]).astype(BF)
        return 0

    lax.fori_loop(0, out_ref.shape[0] // 16, body, 0)


def down_rows(key_ref, map_ref, weight_ref, hid_ref, out_ref, snap_ref, odd):
    upright(key_ref, snap_ref)
    rank, width = map_ref.shape[0], weight_ref.shape[1]
    column = lax.broadcasted_iota(jnp.int32, (1, rank), 1)
    source = lax.broadcasted_iota(jnp.int32, (rank, 128), 0)
    lane = lax.broadcasted_iota(jnp.int32, (rank, 128), 1)
    fold = jnp.where(lane % 64 == source % 8 + 8 * lax.axis_index(ROWS), 1.0, 0.0).astype(BF)
    group = BLOCK // 32

    def body(i, _):
        at = strip(i, BLOCK)
        hidden = hid_ref[at, :] if len(hid_ref.shape) == 2 else hid_ref[odd, at, :]
        blocks = [2 * (group * i + q) + odd for q in range(group)]
        snap = jnp.concatenate(
            [snap_ref[pl.ds(pl.multiple_of(32 * b, 32), 32), :] for b in blocks], axis=0
        )[:, :1]
        wide = jnp.where(column // 8 == snap, _dot_nt(hidden, map_ref[...]), 0.0).astype(BF)
        ranks = _dot(wide, fold).astype(BF)
        total = _dot(hidden, weight_ref[...]).astype(BF)
        for q, b in enumerate(blocks):
            rows = pl.ds(pl.multiple_of(leaves_to(b) * 32, 32), 32)
            out_ref[rows, :width] = total[32 * q : 32 * q + 32]
            out_ref[rows, width:] = ranks[32 * q : 32 * q + 32]
        return 0

    lax.fori_loop(0, out_ref.shape[0] // BLOCK, body, 0)


def down_send_kernel(key_ref, map_ref, weight_ref, *rest):
    pieces, (out_ref, keep_ref, snap_ref, hid_ref) = rest[:16], rest[16:]
    for cols, part in ((slice(0, CUT), pieces[:8]), (slice(CUT, None), pieces[8:])):
        for m, piece in enumerate(part):
            for q in range(4):
                to = 32 * (2 * m + q // 2)
                hid_ref[q % 2, to : to + 32, cols] = piece[32 * q : 32 * q + 32, :]
    core = lax.axis_index(HID) & 1
    keep_ref[...] = hid_ref[core]
    down_rows(key_ref, map_ref, weight_ref, hid_ref, out_ref, snap_ref, 1 - core)


def down_keep_kernel(key_ref, map_ref, weight_ref, hid_ref, out_ref, snap_ref):
    core = lax.axis_index(HID) & 1
    down_rows(key_ref, map_ref, weight_ref, hid_ref, out_ref, snap_ref, core)


def sum_kernel(count, *refs):
    ins, outs = refs[:count], refs[count:]
    n = outs[0].shape[0] // 16
    for k, out_ref in enumerate(outs):

        def body(r, _):
            at = strip(k * n + r, 16)
            out_ref[strip(r, 16), :] = sum(ref[at, :].astype(F32) for ref in ins).astype(BF)
            return 0

        lax.fori_loop(0, n, body, 0)


def last_wave_kernel(a_ref, b_ref, c_ref, d_ref, out_ref, rank_ref):
    total = (
        a_ref[...].astype(F32) + b_ref[...].astype(F32)
        + c_ref[...].astype(F32) + d_ref[...].astype(F32)
    )
    width = out_ref.shape[1]
    out_ref[...] = total[:, :width]
    rank_ref[...] = total[:, width:].astype(BF)


def lift_kernel(mine_ref, total_ref, rank_ref, map_ref, out_ref):
    lane = lax.broadcasted_iota(jnp.int32, mine_ref.shape, 1) >> 6
    pair, mine = jnp.sum(rank_ref[...].astype(F32), axis=0), mine_ref[...]

    def body(i, total):
        spread = jnp.concatenate(
            [jnp.where(lane + 2 * (4 * i + m) == mine, pair, 0.0).astype(BF) for m in range(4)],
            axis=1,
        )
        return total + _dot(spread, map_ref[strip(i, 512), :])

    total = lax.fori_loop(0, map_ref.shape[0] // 512, body, total_ref[...])
    out_ref[...] = total.astype(BF)


def stack(parts):
    rows = sum(p.shape[0] for p in parts)
    return call(
        stack_kernel, parts, ((rows, parts[0].shape[1]), BF), 2, flops=1,
        scratch=[pltpu.SemaphoreType.DMA((len(parts),))], far=range(len(parts)),
    )


def gather_rows(x, later):
    wave = stack([x] + [lax.ppermute(x, HID, FIRST[k]) for k in (1, 2, 3)])
    wave, later = lax.optimization_barrier((wave, later))
    wave = stack([wave] + [lax.ppermute(wave, HID, SECOND[k]) for k in (1, 2, 3)])
    return wave, later


def add_up(parts):
    total = parts[0].astype(F32)
    for part in parts[1:]:
        total = total + part.astype(F32)
    return total


def scatter_rows(keep, send, maps):
    rows, width = keep.shape
    parts = call(
        functools.partial(sum_kernel, 2), (keep, lax.ppermute(send, HID, SIBLING)),
        (((rows // 4, width), BF),) * 4, 4, flops=WAIT,
    )
    parts = [parts[0]] + [lax.ppermute(parts[k], HID, FIRST[k]) for k in (1, 2, 3)]
    parts = call(
        functools.partial(sum_kernel, 4), parts, (((rows // 16, width), BF),) * 4, 4, flops=WAIT
    )
    parts, maps = lax.optimization_barrier((parts, maps))
    return [parts[0]] + [lax.ppermute(parts[k], HID, SECOND[k]) for k in (1, 2, 3)], maps


def reduce_z(streams):
    going = {}
    for step in range(4):
        for g in range(2):
            if (step, g) == (0, 1):
                going[0, -1], streams[1] = lax.optimization_barrier((going[0, -1], streams[1]))
            terms, go_up, go_down = streams[g]
            up_hops, shape = 3 + g, go_up.shape
            for sign, hops, perm in ((-1, 7 - up_hops, DOWN_Z), (1, up_hops, UP_Z)):
                hop = step - (4 - hops)
                if hop < 0:
                    continue
                term = go_up if sign == 1 else go_down
                if hop:
                    add = functools.partial(add_kernel, (sign * (hops - hop)) % NZ)
                    term = call(add, (going[g, sign], terms), (shape, BF), 2, flops=1)
                going[g, sign] = lax.ppermute(term, ROWS, perm)
    return [
        call(
            swiglu_kernel, (going[g, 1], going[g, -1], terms),
            ((go_up.shape[0], go_up.shape[1] // 2), BF), 4, flops=1,
        )
        for g, (terms, go_up, _) in enumerate(streams)
    ]


def gather_z(x, far_up):
    ups, downs = [x], [x]
    for hop in range(4):
        if hop < 3 or far_up:
            ups.append(lax.ppermute(ups[-1], ROWS, UP_Z))
        if hop < 3 or not far_up:
            downs.append(lax.ppermute(downs[-1], ROWS, DOWN_Z))
    return downs + ups[:0:-1]


def per_device(
    tokens, snapshot, gate_weight, up_weight, down_weight, input_maps, middle_maps, down_in, down_out
):
    count = snapshot.shape[0]
    units = gate_weight.shape[1]
    width = tokens.shape[1]
    snaps = middle_maps.shape[0]
    part = count // NZ

    own, middle_maps = gather_rows(tokens, middle_maps)
    key = call(
        key_kernel, (snapshot.reshape(NZ, part),), ((NZ, part), jnp.int32), 2, flops=WAIT,
        scratch=[pltpu.VMEM((NZ, part), jnp.int32)],
    )
    middle = (
        middle_maps.reshape(snaps // 2, 2, 2, 8, units)
        .transpose(2, 1, 0, 3, 4)
        .reshape(2, snaps * 8, units)
    )
    own, key, middle, down_out = lax.optimization_barrier((own, key, middle, down_out))
    sib = lax.ppermute(own, HID, SIBLING)
    down_maps = lax.all_gather(down_out, HID, axis=0, tiled=True)
    ranks, rows = call(
        rank_kernel, (key, own, sib, input_maps),
        (((NZ, 8, 128), F32), ((count, width), BF)), 5, flops=WAIT,
    )
    ranks = add_up(list(lax.all_to_all(ranks, ROWS, 0, 0))).astype(BF)
    ranks = lax.all_to_all(jnp.broadcast_to(ranks[None], (32, 8, 128)), HID, 0, 0)
    def stream(n):
        return ((count, 2 * n), BF), ((part, 2 * n), BF), ((part, 2 * n), BF)

    marks = pltpu.VMEM((count, 128), jnp.int32)
    spread, *early = call(
        first_kernel, (key, ranks.reshape(256, 128), rows, gate_weight, up_weight, middle),
        (((2, count, snaps * 8), BF), *stream(CUT)), 12, flops=5e9, scratch=[marks, marks],
    )
    mine, *late = call(
        second_kernel, (key, rows, spread, gate_weight, up_weight, middle),
        (((32, 128), jnp.int32), *stream(units - CUT)), 10, flops=3e9, scratch=[marks],
    )
    pieces = [
        p for g, hidden in enumerate(reduce_z([early, late])) for p in gather_z(hidden, g == 0)
    ]
    down_in = down_in.reshape(snaps * 8, units)
    half = ((count // 2, width + 128), BF)
    send, hid = call(
        down_send_kernel, (key, down_in, down_weight, *pieces),
        (half, ((count // 2, units), BF)), 10, flops=2e9,
        scratch=[marks, pltpu.VMEM((2, count // 2, units), BF)],
    )
    keep = call(
        down_keep_kernel, (key, down_in, down_weight, hid), half, 10, flops=2e9,
        scratch=[marks],
    )
    parts, down_maps = scatter_rows(keep, send, down_maps)
    total, rank = call(
        last_wave_kernel, parts, (((32, width), F32), ((32, 128), BF)), 4, flops=WAIT
    )
    rank, total = lax.optimization_barrier((rank, total))
    maps = down_maps.reshape(snaps * NZ * 8, width)
    rank = lax.all_to_all(jnp.broadcast_to(rank[None], (NZ, 32, 128)), ROWS, 0, 0)
    return call(lift_kernel, (mine, total, rank, maps), ((32, width), BF), 4, flops=3e8)


def solution(mesh):
    return jax.shard_map(
        per_device,
        mesh=mesh,
        in_specs=(
            P("hidden", "rows"),
            P(),
            P("rows", "hidden"),
            P("rows", "hidden"),
            P("hidden", "rows"),
            P("hidden", "rows", None),
            P(None, None, "rows", "hidden"),
            P(None, "rows", "hidden"),
            P("hidden", None, "rows"),
        ),
        out_specs=P("hidden", "rows"),
        check_vma=False,
    )
```

```python
import functools

import jax
import jax.numpy as jnp
from jax import lax
from jax.experimental import pallas as pl
from jax.experimental.pallas import tpu as pltpu
from jax.sharding import PartitionSpec as P

BF = jnp.bfloat16
F32 = jnp.float32
NX, NY, NZ = 4, 4, 8
ROWS, HID = "rows", "hidden"
BLOCK = 512
WAIT = 4e9
CUT = 512


def _h(x, y, c):
    return (x * NY + y) * 2 + c


def _plane(f):
    return [
        (_h(x, y, c), _h(*f(x, y, c))) for x in range(NX) for y in range(NY) for c in range(2)
    ]


def _on_x(k):
    return lambda x, y, c: ((x + k) % NX, y, c)


def _on_y(k):
    return lambda x, y, c: (x, (y + k) % NY, c)


FIRST = {k: _plane(lambda x, y, c, k=k: (_on_y(k) if c else _on_x(k))(x, y, c)) for k in (1, 2, 3)}
SECOND = {k: _plane(lambda x, y, c, k=k: (_on_x(k) if c else _on_y(k))(x, y, c)) for k in (1, 2, 3)}
SIBLING = _plane(lambda x, y, c: (x, y, 1 - c))
UP_Z = [(i, (i + 1) % NZ) for i in range(NZ)]
DOWN_Z = [(i, (i - 1) % NZ) for i in range(NZ)]


def _dot(a, b):
    return jnp.dot(a, b, preferred_element_type=F32)


def _dot_nt(a, b):
    return lax.dot_general(a, b, (((1,), (1,)), ((), ())), preferred_element_type=F32)


VM = pl.BlockSpec(memory_space=pltpu.VMEM)
ANY = pl.BlockSpec(memory_space=pl.ANY)
SM = pl.BlockSpec(memory_space=pltpu.SMEM)


def call(kernel, args, out, mib, flops, scratch=(), far=()):
    one = not isinstance(out[0][0], tuple)
    shapes = [jax.ShapeDtypeStruct(*o) for o in ([out] if one else out)]
    moved = sum(a.size * a.dtype.itemsize for a in [*args, *shapes])
    return pl.pallas_call(
        kernel,
        out_shape=shapes[0] if one else tuple(shapes),
        in_specs=[SM if a.ndim == 1 else ANY if i in far else VM for i, a in enumerate(args)],
        out_specs=VM if one else (VM,) * len(shapes),
        scratch_shapes=list(scratch),
        compiler_params=pltpu.CompilerParams(vmem_limit_bytes=mib << 20),
        cost_estimate=pl.CostEstimate(
            flops=int(flops), bytes_accessed=moved, transcendentals=0
        ),
        name=getattr(kernel, "func", kernel).__name__,
    )(*args)


def place():
    z, h = lax.axis_index(ROWS), lax.axis_index(HID)
    return z, h >> 3, h >> 1 & 3, h & 1


def arrived_from(p):
    z, x, y, c = place()
    core = c ^ (p >> 4)
    far, near = p >> 2 & 3, p & 3
    ox, oy = (x - jnp.where(core == 0, near, far)) & 3, (y - jnp.where(core == 0, far, near)) & 3
    return (ox * 8 + oy * 2 + core - 4 * z) & 31


def leaves_to(i):
    z, x, y, _ = place()
    h = (i + 4 * z) & 31
    ex, ey = ((h >> 3) - x) & 3, ((h >> 1 & 3) - y) & 3
    return jnp.where(h & 1 == 0, ex * 4 + ey, ey * 4 + ex)


def key_kernel(snap_ref, out_ref, key_ref):
    n = snap_ref.shape[0]
    earlier = lax.broadcasted_iota(jnp.int32, (128, 128), 0) < lax.broadcasted_iota(
        jnp.int32, (128, 128), 1
    )
    columns = [
        jnp.broadcast_to(snap_ref[r : r + 1, :].astype(F32), (128, 128)).T.astype(jnp.int32)
        for r in range(n)
    ]
    for r in range(n):
        row = snap_ref[r : r + 1, :]
        count = jnp.where((columns[r] == row) & earlier, 1, 0)
        for q in range(r):
            count += jnp.where(columns[q] == row, 1, 0)
        key_ref[r : r + 1, :] = row * 32 + jnp.sum(count, axis=0, keepdims=True)
    z = lax.axis_index(ROWS)
    for i in range(n):
        out_ref[i : i + 1, :] = key_ref[pl.ds((z + i) & (n - 1), 1), :]


def stack_kernel(*refs):
    *ins, out_ref, sems = refs
    copies, row = [], 0
    for i, ref in enumerate(ins):
        to = out_ref.at[pl.ds(row, ref.shape[0])]
        copies.append(pltpu.make_async_copy(ref, to, sems.at[i]))
        row += ref.shape[0]
    for copy in copies:
        copy.start()
    for copy in copies:
        copy.wait()


def rank_kernel(key_ref, own_ref, sib_ref, maps_ref, out_ref, rows_ref):
    for p in range(32):
        source = own_ref if p < 16 else sib_ref
        rows_ref[strip(arrived_from(p), 32), :] = source[p % 16 * 32 : p % 16 * 32 + 32, :]
    wanted = 64 * lax.axis_index(HID) + lax.broadcasted_iota(jnp.int32, (64, 128), 0)
    pick = jnp.concatenate(
        [
            jnp.where(key_ref[i : i + 1, :] == wanted, 1.0, 0.0).astype(BF)
            for i in range(key_ref.shape[0])
        ],
        axis=1,
    )
    picked = _dot(pick, rows_ref[...]).astype(BF)
    cap = picked.shape[0] // 2
    ranks = jnp.concatenate(
        [_dot(picked[i * cap : (i + 1) * cap], maps_ref[i]) for i in range(2)], axis=0
    )
    turned = ranks.T
    blocks, k = out_ref.shape[0], out_ref.shape[1]
    side = blocks * k
    for r in range(blocks):
        at = slice(r * k, r * k + k)
        out_ref[r] = jnp.concatenate([turned[:side][at], turned[side:][at]], axis=1)


def upright(key_ref, snap_ref, slot_ref=None):
    n = key_ref.shape[1]
    for i in range(key_ref.shape[0]):
        key = jnp.broadcast_to(key_ref[i : i + 1, :].astype(F32), (n, n)).T.astype(jnp.int32)
        snap_ref[i * n : (i + 1) * n, :] = key >> 5
        if slot_ref is not None:
            slot_ref[i * n : (i + 1) * n, :] = key & 31


def in_blocks(count, rows, body):
    lax.fori_loop(
        0, count // rows, lambda i, _: body(pl.ds(pl.multiple_of(i * rows, rows), rows)) or 0, 0
    )


def send_copies(all_ref, up_ref, down_ref, up_hops):
    rows = up_ref.shape[0]
    for ref, i in ((up_ref, up_hops), (down_ref, 1 + up_hops)):
        ref[...] = all_ref[i * rows : (i + 1) * rows, :]


def first_kernel(
    key_ref, ranks_ref, rows_ref, gate_ref, up_ref, mid_ref,
    spread_ref, all_ref, go_up_ref, go_down_ref, snap_ref, slot_ref,
):
    upright(key_ref, snap_ref, slot_ref)
    column = lax.broadcasted_iota(jnp.int32, (1, 256), 1)

    def body(at):
        snap, slot = snap_ref[at, :1], slot_ref[at, :]
        lane = lax.broadcasted_iota(jnp.int32, slot.shape, 1)
        for j, weight_ref in enumerate((gate_ref, up_ref)):
            spread = []
            for l in range(2):
                hot = jnp.where(lane == slot + 32 * (2 * j + l), 1.0, 0.0).astype(BF)
                wide = _dot_nt(hot, ranks_ref[...])
                spread.append(jnp.where(2 * (column // 8) + l == snap, wide, 0.0).astype(BF))
            spread = jnp.concatenate(spread, axis=1)
            spread_ref[j, at, :] = spread
            total = _dot(rows_ref[at, :], weight_ref[:, :CUT]) + _dot(spread, mid_ref[j, :, :CUT])
            all_ref[at, j * CUT : (j + 1) * CUT] = total.astype(BF)

    in_blocks(rows_ref.shape[0], BLOCK, body)
    send_copies(all_ref, go_up_ref, go_down_ref, 3)


def second_kernel(
    key_ref, rows_ref, spread_ref, gate_ref, up_ref, mid_ref,
    mine_ref, all_ref, go_up_ref, go_down_ref, snap_ref,
):
    upright(key_ref, snap_ref)
    block = (lax.axis_index(HID) - 4 * lax.axis_index(ROWS)) & 31
    mine_ref[...] = snap_ref[pl.ds(pl.multiple_of(block * 32, 32), 32), :]
    n = all_ref.shape[1] // 2

    def body(at):
        for j, weight_ref in enumerate((gate_ref, up_ref)):
            total = _dot(rows_ref[at, :], weight_ref[:, CUT:])
            total += _dot(spread_ref[j, at, :], mid_ref[j, :, CUT:])
            all_ref[at, j * n : (j + 1) * n] = total.astype(BF)

    in_blocks(rows_ref.shape[0], BLOCK, body)
    send_copies(all_ref, go_up_ref, go_down_ref, 4)


def strip(i, rows):
    return pl.ds(pl.multiple_of(i * rows, rows), rows)


def add_kernel(i, a_ref, all_ref, out_ref):
    n = out_ref.shape[0] // 16

    def body(r, _):
        at = strip(r, 16)
        own = all_ref[strip(i * n + r, 16), :]
        out_ref[at, :] = (a_ref[at, :].astype(F32) + own.astype(F32)).astype(BF)
        return 0

    lax.fori_loop(0, n, body, 0)


def swiglu_kernel(a_ref, b_ref, all_ref, out_ref):
    n = out_ref.shape[1]

    def body(r, _):
        at = strip(r, 16)
        total = a_ref[at, :].astype(F32) + b_ref[at, :].astype(F32) + all_ref[at, :].astype(F32)
        gate = total[:, :n]
        out_ref[at, :] = (gate / (1.0 + jnp.exp(-gate)) * total[:, n:]).astype(BF)
        return 0

    lax.fori_loop(0, out_ref.shape[0] // 16, body, 0)


def down_rows(key_ref, map_ref, weight_ref, hid_ref, out_ref, snap_ref, odd):
    upright(key_ref, snap_ref)
    rank, width = map_ref.shape[0], weight_ref.shape[1]
    column = lax.broadcasted_iota(jnp.int32, (1, rank), 1)
    source = lax.broadcasted_iota(jnp.int32, (rank, 128), 0)
    lane = lax.broadcasted_iota(jnp.int32, (rank, 128), 1)
    fold = jnp.where(lane % 64 == source % 8 + 8 * lax.axis_index(ROWS), 1.0, 0.0).astype(BF)
    group = BLOCK // 32

    def body(i, _):
        at = strip(i, BLOCK)
        hidden = hid_ref[at, :] if len(hid_ref.shape) == 2 else hid_ref[odd, at, :]
        blocks = [2 * (group * i + q) + odd for q in range(group)]
        snap = jnp.concatenate(
            [snap_ref[pl.ds(pl.multiple_of(32 * b, 32), 32), :] for b in blocks], axis=0
        )[:, :1]
        wide = jnp.where(column // 8 == snap, _dot_nt(hidden, map_ref[...]), 0.0).astype(BF)
        ranks = _dot(wide, fold).astype(BF)
        total = _dot(hidden, weight_ref[...]).astype(BF)
        for q, b in enumerate(blocks):
            rows = pl.ds(pl.multiple_of(leaves_to(b) * 32, 32), 32)
            out_ref[rows, :width] = total[32 * q : 32 * q + 32]
            out_ref[rows, width:] = ranks[32 * q : 32 * q + 32]
        return 0

    lax.fori_loop(0, out_ref.shape[0] // BLOCK, body, 0)


def down_send_kernel(key_ref, map_ref, weight_ref, *rest):
    pieces, (out_ref, keep_ref, snap_ref, hid_ref) = rest[:16], rest[16:]
    for cols, part in ((slice(0, CUT), pieces[:8]), (slice(CUT, None), pieces[8:])):
        for m, piece in enumerate(part):
            for q in range(4):
                to = 32 * (2 * m + q // 2)
                hid_ref[q % 2, to : to + 32, cols] = piece[32 * q : 32 * q + 32, :]
    core = lax.axis_index(HID) & 1
    keep_ref[...] = hid_ref[core]
    down_rows(key_ref, map_ref, weight_ref, hid_ref, out_ref, snap_ref, 1 - core)


def down_keep_kernel(key_ref, map_ref, weight_ref, hid_ref, out_ref, snap_ref):
    core = lax.axis_index(HID) & 1
    down_rows(key_ref, map_ref, weight_ref, hid_ref, out_ref, snap_ref, core)


def sum_kernel(count, *refs):
    ins, outs = refs[:count], refs[count:]
    n = outs[0].shape[0] // 16
    for k, out_ref in enumerate(outs):

        def body(r, _):
            at = strip(k * n + r, 16)
            out_ref[strip(r, 16), :] = sum(ref[at, :].astype(F32) for ref in ins).astype(BF)
            return 0

        lax.fori_loop(0, n, body, 0)


def last_wave_kernel(a_ref, b_ref, c_ref, d_ref, out_ref, rank_ref):
    total = (
        a_ref[...].astype(F32) + b_ref[...].astype(F32)
        + c_ref[...].astype(F32) + d_ref[...].astype(F32)
    )
    width = out_ref.shape[1]
    out_ref[...] = total[:, :width]
    rank_ref[...] = total[:, width:].astype(BF)


def lift_kernel(mine_ref, total_ref, rank_ref, map_ref, out_ref):
    lane = lax.broadcasted_iota(jnp.int32, mine_ref.shape, 1) >> 6
    pair, mine = jnp.sum(rank_ref[...].astype(F32), axis=0), mine_ref[...]

    spread = jnp.concatenate(
        [
            jnp.where(lane + 2 * m == mine, pair, 0.0).astype(BF)
            for m in range(map_ref.shape[0] // 128)
        ],
        axis=1,
    )
    out_ref[...] = (total_ref[...] + _dot(spread, map_ref[...])).astype(BF)


def stack(parts):
    rows = sum(p.shape[0] for p in parts)
    return call(
        stack_kernel, parts, ((rows, parts[0].shape[1]), BF), 2, flops=1,
        scratch=[pltpu.SemaphoreType.DMA((len(parts),))], far=range(len(parts)),
    )


def gather_rows(x, later):
    wave = stack([x] + [lax.ppermute(x, HID, FIRST[k]) for k in (1, 2, 3)])
    wave, later = lax.optimization_barrier((wave, later))
    wave = stack([wave] + [lax.ppermute(wave, HID, SECOND[k]) for k in (1, 2, 3)])
    return wave, later


def add_up(parts):
    total = parts[0].astype(F32)
    for part in parts[1:]:
        total = total + part.astype(F32)
    return total


def scatter_rows(keep, send, maps):
    rows, width = keep.shape
    parts = call(
        functools.partial(sum_kernel, 2), (keep, lax.ppermute(send, HID, SIBLING)),
        (((rows // 4, width), BF),) * 4, 4, flops=WAIT,
    )
    parts = [parts[0]] + [lax.ppermute(parts[k], HID, FIRST[k]) for k in (1, 2, 3)]
    parts = call(
        functools.partial(sum_kernel, 4), parts, (((rows // 16, width), BF),) * 4, 4, flops=WAIT
    )
    parts, maps = lax.optimization_barrier((parts, maps))
    return [parts[0]] + [lax.ppermute(parts[k], HID, SECOND[k]) for k in (1, 2, 3)], maps


def reduce_z(streams):
    going = {}
    for step in range(4):
        for g in range(2):
            if (step, g) == (0, 1):
                going[0, -1], streams[1] = lax.optimization_barrier((going[0, -1], streams[1]))
            terms, go_up, go_down = streams[g]
            up_hops, shape = 3 + g, go_up.shape
            for sign, hops, perm in ((-1, 7 - up_hops, DOWN_Z), (1, up_hops, UP_Z)):
                hop = step - (4 - hops)
                if hop < 0:
                    continue
                term = go_up if sign == 1 else go_down
                if hop:
                    add = functools.partial(add_kernel, (sign * (hops - hop)) % NZ)
                    term = call(add, (going[g, sign], terms), (shape, BF), 2, flops=1)
                going[g, sign] = lax.ppermute(term, ROWS, perm)
    return [
        call(
            swiglu_kernel, (going[g, 1], going[g, -1], terms),
            ((go_up.shape[0], go_up.shape[1] // 2), BF), 4, flops=1,
        )
        for g, (terms, go_up, _) in enumerate(streams)
    ]


def gather_z(x, far_up):
    ups, downs = [x], [x]
    for hop in range(4):
        if hop < 3 or far_up:
            ups.append(lax.ppermute(ups[-1], ROWS, UP_Z))
        if hop < 3 or not far_up:
            downs.append(lax.ppermute(downs[-1], ROWS, DOWN_Z))
    return downs + ups[:0:-1]


def per_device(
    tokens, snapshot, gate_weight, up_weight, down_weight, input_maps, middle_maps, down_in, down_out
):
    count = snapshot.shape[0]
    units = gate_weight.shape[1]
    width = tokens.shape[1]
    snaps = middle_maps.shape[0]
    part = count // NZ

    own, middle_maps = gather_rows(tokens, middle_maps)
    key = call(
        key_kernel, (snapshot.reshape(NZ, part),), ((NZ, part), jnp.int32), 2, flops=WAIT,
        scratch=[pltpu.VMEM((NZ, part), jnp.int32)],
    )
    middle = (
        middle_maps.reshape(snaps // 2, 2, 2, 8, units)
        .transpose(2, 1, 0, 3, 4)
        .reshape(2, snaps * 8, units)
    )
    own, key, middle, down_out = lax.optimization_barrier((own, key, middle, down_out))
    sib = lax.ppermute(own, HID, SIBLING)
    down_maps = lax.all_gather(down_out, HID, axis=0, tiled=True)
    ranks, rows = call(
        rank_kernel, (key, own, sib, input_maps),
        (((NZ, 8, 128), F32), ((count, width), BF)), 5, flops=WAIT,
    )
    ranks = add_up(list(lax.all_to_all(ranks, ROWS, 0, 0))).astype(BF)
    ranks = lax.all_to_all(jnp.broadcast_to(ranks[None], (32, 8, 128)), HID, 0, 0)
    def stream(n):
        return ((count, 2 * n), BF), ((part, 2 * n), BF), ((part, 2 * n), BF)

    marks = pltpu.VMEM((count, 128), jnp.int32)
    spread, *early = call(
        first_kernel, (key, ranks.reshape(256, 128), rows, gate_weight, up_weight, middle),
        (((2, count, snaps * 8), BF), *stream(CUT)), 12, flops=5e9, scratch=[marks, marks],
    )
    mine, *late = call(
        second_kernel, (key, rows, spread, gate_weight, up_weight, middle),
        (((32, 128), jnp.int32), *stream(units - CUT)), 10, flops=3e9, scratch=[marks],
    )
    pieces = [
        p for g, hidden in enumerate(reduce_z([early, late])) for p in gather_z(hidden, g == 0)
    ]
    down_in = down_in.reshape(snaps * 8, units)
    half = ((count // 2, width + 128), BF)
    send, hid = call(
        down_send_kernel, (key, down_in, down_weight, *pieces),
        (half, ((count // 2, units), BF)), 10, flops=2e9,
        scratch=[marks, pltpu.VMEM((2, count // 2, units), BF)],
    )
    keep = call(
        down_keep_kernel, (key, down_in, down_weight, hid), half, 10, flops=2e9,
        scratch=[marks],
    )
    parts, down_maps = scatter_rows(keep, send, down_maps)
    total, rank = call(
        last_wave_kernel, parts, (((32, width), F32), ((32, 128), BF)), 4, flops=WAIT
    )
    rank, total = lax.optimization_barrier((rank, total))
    maps = down_maps.reshape(snaps * NZ * 8, width)
    rank = lax.all_to_all(jnp.broadcast_to(rank[None], (NZ, 32, 128)), ROWS, 0, 0)
    return call(lift_kernel, (mine, total, rank, maps), ((32, width), BF), 4, flops=3e8)


def solution(mesh):
    return jax.shard_map(
        per_device,
        mesh=mesh,
        in_specs=(
            P("hidden", "rows"),
            P(),
            P("rows", "hidden"),
            P("rows", "hidden"),
            P("hidden", "rows"),
            P("hidden", "rows", None),
            P(None, None, "rows", "hidden"),
            P(None, "rows", "hidden"),
            P("hidden", None, "rows"),
        ),
        out_specs=P("hidden", "rows"),
        check_vma=False,
    )
```

```python
import functools

import jax
import jax.numpy as jnp
from jax import lax
from jax.experimental import pallas as pl
from jax.experimental.pallas import tpu as pltpu
from jax.sharding import PartitionSpec as P

BF = jnp.bfloat16
F32 = jnp.float32
NX, NY, NZ = 4, 4, 8
ROWS, HID = "rows", "hidden"
BLOCK = 512
WAIT = 4e9
CUT = 384


def _h(x, y, c):
    return (x * NY + y) * 2 + c


def _plane(f):
    return [
        (_h(x, y, c), _h(*f(x, y, c))) for x in range(NX) for y in range(NY) for c in range(2)
    ]


def _on_x(k):
    return lambda x, y, c: ((x + k) % NX, y, c)


def _on_y(k):
    return lambda x, y, c: (x, (y + k) % NY, c)


FIRST = {k: _plane(lambda x, y, c, k=k: (_on_y(k) if c else _on_x(k))(x, y, c)) for k in (1, 2, 3)}
SECOND = {k: _plane(lambda x, y, c, k=k: (_on_x(k) if c else _on_y(k))(x, y, c)) for k in (1, 2, 3)}
SIBLING = _plane(lambda x, y, c: (x, y, 1 - c))
UP_Z = [(i, (i + 1) % NZ) for i in range(NZ)]
DOWN_Z = [(i, (i - 1) % NZ) for i in range(NZ)]


def _dot(a, b):
    return jnp.dot(a, b, preferred_element_type=F32)


def _dot_nt(a, b):
    return lax.dot_general(a, b, (((1,), (1,)), ((), ())), preferred_element_type=F32)


VM = pl.BlockSpec(memory_space=pltpu.VMEM)
ANY = pl.BlockSpec(memory_space=pl.ANY)
SM = pl.BlockSpec(memory_space=pltpu.SMEM)


def call(kernel, args, out, mib, flops, scratch=(), far=()):
    one = not isinstance(out[0][0], tuple)
    shapes = [jax.ShapeDtypeStruct(*o) for o in ([out] if one else out)]
    moved = sum(a.size * a.dtype.itemsize for a in [*args, *shapes])
    return pl.pallas_call(
        kernel,
        out_shape=shapes[0] if one else tuple(shapes),
        in_specs=[SM if a.ndim == 1 else ANY if i in far else VM for i, a in enumerate(args)],
        out_specs=VM if one else (VM,) * len(shapes),
        scratch_shapes=list(scratch),
        compiler_params=pltpu.CompilerParams(vmem_limit_bytes=mib << 20),
        cost_estimate=pl.CostEstimate(
            flops=int(flops), bytes_accessed=moved, transcendentals=0
        ),
        name=getattr(kernel, "func", kernel).__name__,
    )(*args)


def place():
    z, h = lax.axis_index(ROWS), lax.axis_index(HID)
    return z, h >> 3, h >> 1 & 3, h & 1


def arrived_from(p):
    z, x, y, c = place()
    core = c ^ (p >> 4)
    far, near = p >> 2 & 3, p & 3
    ox, oy = (x - jnp.where(core == 0, near, far)) & 3, (y - jnp.where(core == 0, far, near)) & 3
    return (ox * 8 + oy * 2 + core - 4 * z) & 31


def leaves_to(i):
    z, x, y, _ = place()
    h = (i + 4 * z) & 31
    ex, ey = ((h >> 3) - x) & 3, ((h >> 1 & 3) - y) & 3
    return jnp.where(h & 1 == 0, ex * 4 + ey, ey * 4 + ex)


def key_kernel(snap_ref, out_ref, key_ref):
    n = snap_ref.shape[0]
    earlier = lax.broadcasted_iota(jnp.int32, (128, 128), 0) < lax.broadcasted_iota(
        jnp.int32, (128, 128), 1
    )
    columns = [
        jnp.broadcast_to(snap_ref[r : r + 1, :].astype(F32), (128, 128)).T.astype(jnp.int32)
        for r in range(n)
    ]
    for r in range(n):
        row = snap_ref[r : r + 1, :]
        count = jnp.where((columns[r] == row) & earlier, 1, 0)
        for q in range(r):
            count += jnp.where(columns[q] == row, 1, 0)
        key_ref[r : r + 1, :] = row * 32 + jnp.sum(count, axis=0, keepdims=True)
    z = lax.axis_index(ROWS)
    for i in range(n):
        out_ref[i : i + 1, :] = key_ref[pl.ds((z + i) & (n - 1), 1), :]


def stack_kernel(*refs):
    *ins, out_ref, sems = refs
    copies, row = [], 0
    for i, ref in enumerate(ins):
        to = out_ref.at[pl.ds(row, ref.shape[0])]
        copies.append(pltpu.make_async_copy(ref, to, sems.at[i]))
        row += ref.shape[0]
    for copy in copies:
        copy.start()
    for copy in copies:
        copy.wait()


def rank_kernel(key_ref, own_ref, sib_ref, maps_ref, out_ref, rows_ref):
    for p in range(32):
        source = own_ref if p < 16 else sib_ref
        rows_ref[strip(arrived_from(p), 32), :] = source[p % 16 * 32 : p % 16 * 32 + 32, :]
    wanted = 64 * lax.axis_index(HID) + lax.broadcasted_iota(jnp.int32, (64, 128), 0)
    pick = jnp.concatenate(
        [
            jnp.where(key_ref[i : i + 1, :] == wanted, 1.0, 0.0).astype(BF)
            for i in range(key_ref.shape[0])
        ],
        axis=1,
    )
    picked = _dot(pick, rows_ref[...]).astype(BF)
    cap = picked.shape[0] // 2
    ranks = jnp.concatenate(
        [_dot(picked[i * cap : (i + 1) * cap], maps_ref[i]) for i in range(2)], axis=0
    )
    turned = ranks.T
    blocks, k = out_ref.shape[0], out_ref.shape[1]
    side = blocks * k
    for r in range(blocks):
        at = slice(r * k, r * k + k)
        out_ref[r] = jnp.concatenate([turned[:side][at], turned[side:][at]], axis=1)


def upright(key_ref, snap_ref, slot_ref=None):
    n = key_ref.shape[1]
    for i in range(key_ref.shape[0]):
        key = jnp.broadcast_to(key_ref[i : i + 1, :].astype(F32), (n, n)).T.astype(jnp.int32)
        snap_ref[i * n : (i + 1) * n, :] = key >> 5
        if slot_ref is not None:
            slot_ref[i * n : (i + 1) * n, :] = key & 31


def in_blocks(count, rows, body):
    lax.fori_loop(
        0, count // rows, lambda i, _: body(pl.ds(pl.multiple_of(i * rows, rows), rows)) or 0, 0
    )


def send_copies(all_ref, up_ref, down_ref, up_hops):
    rows = up_ref.shape[0]
    for ref, i in ((up_ref, up_hops), (down_ref, 1 + up_hops)):
        ref[...] = all_ref[i * rows : (i + 1) * rows, :]


def first_kernel(
    key_ref, ranks_ref, rows_ref, gate_ref, up_ref, mid_ref,
    spread_ref, all_ref, go_up_ref, go_down_ref, snap_ref, slot_ref,
):
    upright(key_ref, snap_ref, slot_ref)
    column = lax.broadcasted_iota(jnp.int32, (1, 256), 1)

    def body(at):
        snap, slot = snap_ref[at, :1], slot_ref[at, :]
        lane = lax.broadcasted_iota(jnp.int32, slot.shape, 1)
        for j, weight_ref in enumerate((gate_ref, up_ref)):
            spread = []
            for l in range(2):
                hot = jnp.where(lane == slot + 32 * (2 * j + l), 1.0, 0.0).astype(BF)
                wide = _dot_nt(hot, ranks_ref[...])
                spread.append(jnp.where(2 * (column // 8) + l == snap, wide, 0.0).astype(BF))
            spread = jnp.concatenate(spread, axis=1)
            spread_ref[j, at, :] = spread
            total = _dot(rows_ref[at, :], weight_ref[:, :CUT]) + _dot(spread, mid_ref[j, :, :CUT])
            all_ref[at, j * CUT : (j + 1) * CUT] = total.astype(BF)

    in_blocks(rows_ref.shape[0], BLOCK, body)
    send_copies(all_ref, go_up_ref, go_down_ref, 3)


def second_kernel(
    key_ref, rows_ref, spread_ref, gate_ref, up_ref, mid_ref,
    mine_ref, all_ref, go_up_ref, go_down_ref, snap_ref,
):
    upright(key_ref, snap_ref)
    block = (lax.axis_index(HID) - 4 * lax.axis_index(ROWS)) & 31
    mine_ref[...] = snap_ref[pl.ds(pl.multiple_of(block * 32, 32), 32), :]
    n = all_ref.shape[1] // 2

    def body(at):
        for j, weight_ref in enumerate((gate_ref, up_ref)):
            total = _dot(rows_ref[at, :], weight_ref[:, CUT:])
            total += _dot(spread_ref[j, at, :], mid_ref[j, :, CUT:])
            all_ref[at, j * n : (j + 1) * n] = total.astype(BF)

    in_blocks(rows_ref.shape[0], BLOCK, body)
    send_copies(all_ref, go_up_ref, go_down_ref, 4)


def strip(i, rows):
    return pl.ds(pl.multiple_of(i * rows, rows), rows)


def add_kernel(i, a_ref, all_ref, out_ref):
    n = out_ref.shape[0] // 16

    def body(r, _):
        at = strip(r, 16)
        own = all_ref[strip(i * n + r, 16), :]
        out_ref[at, :] = (a_ref[at, :].astype(F32) + own.astype(F32)).astype(BF)
        return 0

    lax.fori_loop(0, n, body, 0)


def swiglu_kernel(a_ref, b_ref, all_ref, out_ref):
    n = out_ref.shape[1]

    def body(r, _):
        at = strip(r, 16)
        total = a_ref[at, :].astype(F32) + b_ref[at, :].astype(F32) + all_ref[at, :].astype(F32)
        gate = total[:, :n]
        out_ref[at, :] = (gate / (1.0 + jnp.exp(-gate)) * total[:, n:]).astype(BF)
        return 0

    lax.fori_loop(0, out_ref.shape[0] // 16, body, 0)


def down_rows(key_ref, map_ref, weight_ref, hid_ref, out_ref, snap_ref, odd):
    upright(key_ref, snap_ref)
    rank, width = map_ref.shape[0], weight_ref.shape[1]
    column = lax.broadcasted_iota(jnp.int32, (1, rank), 1)
    source = lax.broadcasted_iota(jnp.int32, (rank, 128), 0)
    lane = lax.broadcasted_iota(jnp.int32, (rank, 128), 1)
    fold = jnp.where(lane % 64 == source % 8 + 8 * lax.axis_index(ROWS), 1.0, 0.0).astype(BF)
    group = BLOCK // 32

    def body(i, _):
        at = strip(i, BLOCK)
        hidden = hid_ref[at, :] if len(hid_ref.shape) == 2 else hid_ref[odd, at, :]
        blocks = [2 * (group * i + q) + odd for q in range(group)]
        snap = jnp.concatenate(
            [snap_ref[pl.ds(pl.multiple_of(32 * b, 32), 32), :] for b in blocks], axis=0
        )[:, :1]
        wide = jnp.where(column // 8 == snap, _dot_nt(hidden, map_ref[...]), 0.0).astype(BF)
        ranks = _dot(wide, fold).astype(BF)
        total = _dot(hidden, weight_ref[...]).astype(BF)
        for q, b in enumerate(blocks):
            rows = pl.ds(pl.multiple_of(leaves_to(b) * 32, 32), 32)
            out_ref[rows, :width] = total[32 * q : 32 * q + 32]
            out_ref[rows, width:] = ranks[32 * q : 32 * q + 32]
        return 0

    lax.fori_loop(0, out_ref.shape[0] // BLOCK, body, 0)


def down_send_kernel(key_ref, map_ref, weight_ref, *rest):
    pieces, (out_ref, keep_ref, snap_ref, hid_ref) = rest[:16], rest[16:]
    for cols, part in ((slice(0, CUT), pieces[:8]), (slice(CUT, None), pieces[8:])):
        for m, piece in enumerate(part):
            for q in range(4):
                to = 32 * (2 * m + q // 2)
                hid_ref[q % 2, to : to + 32, cols] = piece[32 * q : 32 * q + 32, :]
    core = lax.axis_index(HID) & 1
    keep_ref[...] = hid_ref[core]
    down_rows(key_ref, map_ref, weight_ref, hid_ref, out_ref, snap_ref, 1 - core)


def down_keep_kernel(key_ref, map_ref, weight_ref, hid_ref, out_ref, snap_ref):
    core = lax.axis_index(HID) & 1
    down_rows(key_ref, map_ref, weight_ref, hid_ref, out_ref, snap_ref, core)


def sum_kernel(count, *refs):
    ins, outs = refs[:count], refs[count:]
    n = outs[0].shape[0] // 16
    for k, out_ref in enumerate(outs):

        def body(r, _):
            at = strip(k * n + r, 16)
            out_ref[strip(r, 16), :] = sum(ref[at, :].astype(F32) for ref in ins).astype(BF)
            return 0

        lax.fori_loop(0, n, body, 0)


def last_wave_kernel(a_ref, b_ref, c_ref, d_ref, out_ref, rank_ref):
    total = (
        a_ref[...].astype(F32) + b_ref[...].astype(F32)
        + c_ref[...].astype(F32) + d_ref[...].astype(F32)
    )
    width = out_ref.shape[1]
    out_ref[...] = total[:, :width]
    rank_ref[...] = total[:, width:].astype(BF)


def lift_kernel(mine_ref, total_ref, rank_ref, map_ref, out_ref):
    lane = lax.broadcasted_iota(jnp.int32, mine_ref.shape, 1) >> 6
    pair, mine = jnp.sum(rank_ref[...].astype(F32), axis=0), mine_ref[...]

    spread = jnp.concatenate(
        [
            jnp.where(lane + 2 * m == mine, pair, 0.0).astype(BF)
            for m in range(map_ref.shape[0] // 128)
        ],
        axis=1,
    )
    out_ref[...] = (total_ref[...] + _dot(spread, map_ref[...])).astype(BF)


def stack(parts):
    rows = sum(p.shape[0] for p in parts)
    return call(
        stack_kernel, parts, ((rows, parts[0].shape[1]), BF), 2, flops=1,
        scratch=[pltpu.SemaphoreType.DMA((len(parts),))], far=range(len(parts)),
    )


def gather_rows(x, later):
    wave = stack([x] + [lax.ppermute(x, HID, FIRST[k]) for k in (1, 2, 3)])
    wave, later = lax.optimization_barrier((wave, later))
    wave = stack([wave] + [lax.ppermute(wave, HID, SECOND[k]) for k in (1, 2, 3)])
    return wave, later


def add_up(parts):
    total = parts[0].astype(F32)
    for part in parts[1:]:
        total = total + part.astype(F32)
    return total


def scatter_rows(keep, send, maps):
    rows, width = keep.shape
    parts = call(
        functools.partial(sum_kernel, 2), (keep, lax.ppermute(send, HID, SIBLING)),
        (((rows // 4, width), BF),) * 4, 4, flops=WAIT,
    )
    parts = [parts[0]] + [lax.ppermute(parts[k], HID, FIRST[k]) for k in (1, 2, 3)]
    parts = call(
        functools.partial(sum_kernel, 4), parts, (((rows // 16, width), BF),) * 4, 4, flops=WAIT
    )
    parts, maps = lax.optimization_barrier((parts, maps))
    return [parts[0]] + [lax.ppermute(parts[k], HID, SECOND[k]) for k in (1, 2, 3)], maps


def reduce_z(streams):
    going = {}
    for step in range(4):
        for g in range(2):
            if (step, g) == (0, 1):
                going[0, -1], streams[1] = lax.optimization_barrier((going[0, -1], streams[1]))
            terms, go_up, go_down = streams[g]
            up_hops, shape = 3 + g, go_up.shape
            for sign, hops, perm in ((-1, 7 - up_hops, DOWN_Z), (1, up_hops, UP_Z)):
                hop = step - (4 - hops)
                if hop < 0:
                    continue
                term = go_up if sign == 1 else go_down
                if hop:
                    add = functools.partial(add_kernel, (sign * (hops - hop)) % NZ)
                    term = call(add, (going[g, sign], terms), (shape, BF), 2, flops=1)
                going[g, sign] = lax.ppermute(term, ROWS, perm)
    return [
        call(
            swiglu_kernel, (going[g, 1], going[g, -1], terms),
            ((go_up.shape[0], go_up.shape[1] // 2), BF), 4, flops=1,
        )
        for g, (terms, go_up, _) in enumerate(streams)
    ]


def gather_z(x, far_up):
    ups, downs = [x], [x]
    for hop in range(4):
        if hop < 3 or far_up:
            ups.append(lax.ppermute(ups[-1], ROWS, UP_Z))
        if hop < 3 or not far_up:
            downs.append(lax.ppermute(downs[-1], ROWS, DOWN_Z))
    return downs + ups[:0:-1]


def per_device(
    tokens, snapshot, gate_weight, up_weight, down_weight, input_maps, middle_maps, down_in, down_out
):
    count = snapshot.shape[0]
    units = gate_weight.shape[1]
    width = tokens.shape[1]
    snaps = middle_maps.shape[0]
    part = count // NZ

    own, middle_maps = gather_rows(tokens, middle_maps)
    key = call(
        key_kernel, (snapshot.reshape(NZ, part),), ((NZ, part), jnp.int32), 2, flops=WAIT,
        scratch=[pltpu.VMEM((NZ, part), jnp.int32)],
    )
    middle = (
        middle_maps.reshape(snaps // 2, 2, 2, 8, units)
        .transpose(2, 1, 0, 3, 4)
        .reshape(2, snaps * 8, units)
    )
    own, key, middle, down_out = lax.optimization_barrier((own, key, middle, down_out))
    sib = lax.ppermute(own, HID, SIBLING)
    down_maps = lax.all_gather(down_out, HID, axis=0, tiled=True)
    ranks, rows = call(
        rank_kernel, (key, own, sib, input_maps),
        (((NZ, 8, 128), F32), ((count, width), BF)), 5, flops=WAIT,
    )
    ranks = add_up(list(lax.all_to_all(ranks, ROWS, 0, 0))).astype(BF)
    ranks = lax.all_to_all(jnp.broadcast_to(ranks[None], (32, 8, 128)), HID, 0, 0)
    def stream(n):
        return ((count, 2 * n), BF), ((part, 2 * n), BF), ((part, 2 * n), BF)

    marks = pltpu.VMEM((count, 128), jnp.int32)
    spread, *early = call(
        first_kernel, (key, ranks.reshape(256, 128), rows, gate_weight, up_weight, middle),
        (((2, count, snaps * 8), BF), *stream(CUT)), 12, flops=5e9, scratch=[marks, marks],
    )
    mine, *late = call(
        second_kernel, (key, rows, spread, gate_weight, up_weight, middle),
        (((32, 128), jnp.int32), *stream(units - CUT)), 10, flops=3e9, scratch=[marks],
    )
    pieces = [
        p for g, hidden in enumerate(reduce_z([early, late])) for p in gather_z(hidden, g == 0)
    ]
    down_in = down_in.reshape(snaps * 8, units)
    half = ((count // 2, width + 128), BF)
    send, hid = call(
        down_send_kernel, (key, down_in, down_weight, *pieces),
        (half, ((count // 2, units), BF)), 10, flops=2e9,
        scratch=[marks, pltpu.VMEM((2, count // 2, units), BF)],
    )
    keep = call(
        down_keep_kernel, (key, down_in, down_weight, hid), half, 10, flops=2e9,
        scratch=[marks],
    )
    parts, down_maps = scatter_rows(keep, send, down_maps)
    total, rank = call(
        last_wave_kernel, parts, (((32, width), F32), ((32, 128), BF)), 4, flops=WAIT
    )
    rank, total = lax.optimization_barrier((rank, total))
    maps = down_maps.reshape(snaps * NZ * 8, width)
    rank = lax.all_to_all(jnp.broadcast_to(rank[None], (NZ, 32, 128)), ROWS, 0, 0)
    return call(lift_kernel, (mine, total, rank, maps), ((32, width), BF), 4, flops=3e8)


def solution(mesh):
    return jax.shard_map(
        per_device,
        mesh=mesh,
        in_specs=(
            P("hidden", "rows"),
            P(),
            P("rows", "hidden"),
            P("rows", "hidden"),
            P("hidden", "rows"),
            P("hidden", "rows", None),
            P(None, None, "rows", "hidden"),
            P(None, "rows", "hidden"),
            P("hidden", None, "rows"),
        ),
        out_specs=P("hidden", "rows"),
        check_vma=False,
    )
```
